128 devices in a mesh: sec: 4 (over z_hi, core), dp: 32 (over y, x, z_lo).
Axes of the slice: x: 4, y: 4, z: 4 (z_hi: 2, z_lo: 2; z = z_hi * 2 + z_lo), core: 2. Of those that a mesh axis runs over, the one named last changes fastest.
Arguments:
- candidate_hidden_states: bfloat16 [64, 128, 2048], P('dp'), may hold values from -6 to 6
- kept_candidate_index: int32 [64, 128], P('dp'), may hold values from 0 to 127, each once within a row
- slot_parent_beam: int32 [64, 128], P('dp'), may hold values from 0 to 127
- alive_slot_counts: int32 [64], P('dp'), may hold values from 64 to 128, as said below
- slot_expert_index: int32 [64, 128, 2], P('dp'), may hold values from 0 to 31, all different within a row; in each aligned block of 256 rows (0 to 255, 256 to 511, ..., all dimensions but the last counted through in order) at most 24 rows name the same one
- attention_norm_gain: float32 [2048], replicated, may hold values from 0.1 to 1.9
- query_projection_weight: bfloat16 [2048, 2048], P(None, 'sec'), may hold values from -0.125 to 0.125
- key_projection_weight: bfloat16 [2048, 2048], P(None, 'sec'), may hold values from -0.4375 to 0.4375
- value_projection_weight: bfloat16 [2048, 2048], P(None, 'sec'), may hold values from -0.125 to 0.125
- attention_output_weight: bfloat16 [2048, 2048], P('sec'), may hold values from -0.125 to 0.125
- history_event_keys: bfloat16 [64, 2048, 2048], P('dp', None, 'sec'), may hold values from -48 to 48
- history_event_values: bfloat16 [64, 2048, 2048], P('dp', None, 'sec'), may hold values from -6 to 6
- decoded_beam_keys: bfloat16 [64, 128, 2, 2048], P('dp', None, None, 'sec'), may hold values from -16 to 16
- decoded_beam_values: bfloat16 [64, 128, 2, 2048], P('dp', None, None, 'sec'), may hold values from -6 to 6
- expert_norm_gain: float32 [2048], replicated, may hold values from 0.1 to 1.9
- router_projection_weight: bfloat16 [2048, 32], replicated, may hold values from -0.125 to 0.125
- expert_gate_weight: bfloat16 [32, 2048, 2048], P('dp', None, 'sec'), may hold values from -0.125 to 0.125
- expert_up_weight: bfloat16 [32, 2048, 2048], P('dp', None, 'sec'), may hold values from -0.125 to 0.125
- expert_down_weight: bfloat16 [32, 2048, 2048], P('dp', 'sec'), may hold values from -0.125 to 0.125
Outputs:
- output: bfloat16 [64, 128, 2048], P('dp', None, 'sec')
The draws below stay inside these ranges and needn't reach their ends.
Inputs may be any that keep to these rules, and one draw needn't show every extreme that they name: The first alive_slot_counts[u] slots of user u are live; at least one user has all 128 slots live and one has 64. `kept_candidate_index`: each user's row lists every candidate once. `slot_expert_index`: the 2 experts of a slot differ; among the 256 slots of one index of dp (dead slots included) no expert is named more than 24 times, and in every draw some index of dp has an expert named exactly 24 times.
All inputs are finite; a program needn't handle non-finite values.
Results may differ from the reference program's by a relative error of at most 0.012.
Values may be sent and summed in bfloat16 or wider, within the bound.
No kernel may reach another device: no remote copies, remote signals or barrier semaphores. Data moves between devices by JAX's collectives and lax.ppermute only.
A program may use at most 128 MiB of HBM per device.

```python
import math
import jax
import jax.numpy as jnp
import numpy as np
from jax import lax

D = 2048
NH = 16
HD = 128
EH = 2048
TOPK = 2
BEAM_WIDTH = 128
STEPS = 2
H = 2048
ROWS_DEV = 256
USER_TOTAL = 64
EXPERTS = 32
CAP = 24
N_DP = 32


def draw_alive_slot_counts(key, part):
    key = jax.random.fold_in(key, 5)
    counts = jax.random.randint(key, (USER_TOTAL,), BEAM_WIDTH // 2, BEAM_WIDTH + 1, jnp.int32)
    return counts.at[0].set(BEAM_WIDTH).at[USER_TOTAL - 1].set(BEAM_WIDTH // 2)


def draw_history_event_keys(key, part):
    key = jax.random.fold_in(key, 11)
    array_shape = (USER_TOTAL, H, NH * HD)
    values = jnp.clip(jax.random.normal(key, array_shape, jnp.float32) * 0.5, -3.0, 3.0)
    return values.astype(jnp.bfloat16)


def touch_ends(values, own_key, least, high):
    longest = values.shape.index(max(values.shape))
    spots = []
    for shift in (0, 1):
        where = [jax.random.randint(jax.random.fold_in(own_key, axis), (), 0, length) for axis, length in enumerate(values.shape)]
        where[longest] = (where[longest] + shift) % values.shape[longest]
        spots.append(tuple(where))
    return values.at[spots[0]].set(least).at[spots[1]].set(high)


def level_of(key, extent, cuts, low, largest):
    level = 1.0
    for dim, blocks in cuts:
        steps = jax.random.uniform(jax.random.fold_in(jax.random.fold_in(key, 6), dim), (blocks,), jnp.float32, low / len(cuts), largest / len(cuts))
        level = level * jnp.repeat(jnp.exp(steps), extent[dim] // blocks).reshape((-1,) + (1,) * (len(extent) - 1 - dim))
    return level


def assign_block(key, own, number, rows, number_of, top, limit, skew):
    ranking = jax.random.permutation(key, number_of)
    crowded, common = shares(number_of, rows * top, limit, skew, True), shares(number_of, rows * top, limit, skew, False)
    places = jnp.arange(number_of)

    def named(tallies, rotation):
        used = int((tallies > 0).sum())
        fixed = max(1, used // 4)
        moved = fixed + (places - fixed + rotation * (used - fixed)) % max(1, number_of - fixed)
        return jnp.zeros((number_of,), jnp.int32).at[ranking[jnp.where(places < fixed, places, moved)]].set(jnp.asarray(tallies, jnp.int32))

    tallies = jnp.where(number % 4 == 0, named(crowded, number // 4), named(common, number - number // 4 - 1))
    mixed = jax.random.permutation(jax.random.fold_in(own, 3), number_of)
    donor, taker = mixed[0:number_of // 2 * 2:2], mixed[1:number_of // 2 * 2:2]
    slack = jnp.minimum(tallies[donor] - 1, limit - tallies[taker]) // 2
    slack = jnp.where((donor == ranking[0]) | (taker == ranking[0]) | (tallies[taker] == 0), 0, jnp.maximum(slack, 0))
    moved = jax.random.randint(jax.random.fold_in(own, 4), (number_of // 2,), 0, 1 << 20) % (slack + 1)
    tallies = tallies.at[donor].add(-moved).at[taker].add(moved)
    labels = jnp.searchsorted(jnp.cumsum(tallies), jnp.arange(rows * top), side="right").astype(jnp.int32)
    table = labels.reshape(top, rows).T
    table = table[jax.random.permutation(jax.random.fold_in(own, 1), rows)]
    rotation = jax.random.randint(jax.random.fold_in(own, 2), (rows, 1), 0, top)
    return jnp.take_along_axis(table, (jnp.arange(top)[None, :] + rotation) % top, axis=1)


def shares(number_of, total, bound, lean, full):
    loads = [(1 << 20) // math.isqrt(standing ** lean) + 1 for standing in range(1, number_of + 1)]
    largest = bound if full else min(bound, max(-(-total // number_of), total * loads[0] // sum(loads)))
    least = 1 if total - largest >= number_of - 1 else 0
    holding, surplus = [largest] + [least] * (number_of - 1), total - largest - least * (number_of - 1)
    while surplus > 0:
        candidates = [i for i in range(1, number_of) if holding[i] < largest] or [i for i in range(1, number_of) if holding[i] < bound]
        mass, remaining = sum([loads[i] for i in candidates]), surplus
        for i in candidates:
            more = min(bound - holding[i], max(1, remaining * loads[i] // mass), surplus)
            holding[i] = holding[i] + more
            surplus = surplus - more
    return np.array(holding)


def centred(stream_key, shape, width, reach, cuts=(), kind=jnp.bfloat16):
    loudness = level_of(stream_key, shape, cuts, -0.22, 0.18) if cuts else 1.0
    entries = jax.random.normal(stream_key, shape, jnp.float32) * width * loudness
    return jnp.minimum(jnp.maximum(entries, -reach), reach).astype(kind)


def setup_inputs(seed: int = 0) -> dict:
    splits = jax.random.split(jax.random.key(seed), 20)
    candidate_hidden_states = centred(splits[0], (USER_TOTAL, BEAM_WIDTH, D), 1.0, 6.0, ((0, 32),))
    kept_candidate_index = jax.vmap(lambda own: jax.random.permutation(own, BEAM_WIDTH))(jax.random.split(splits[1], USER_TOTAL)).reshape((USER_TOTAL, BEAM_WIDTH)).astype(jnp.int32)
    slot_parent_beam = touch_ends(jax.random.randint(splits[2], (USER_TOTAL, BEAM_WIDTH), 0, BEAM_WIDTH), jax.random.fold_in(splits[2], 1), 0, BEAM_WIDTH - 1).astype(jnp.int32)
    alive_slot_counts = draw_alive_slot_counts(jax.random.fold_in(splits[19], 71), 0)
    slot_expert_index_keys = jax.random.split(jax.random.fold_in(splits[4], 1), USER_TOTAL * BEAM_WIDTH // ROWS_DEV)
    slot_expert_index_turns = jax.random.permutation(jax.random.fold_in(splits[4], 3), USER_TOTAL * BEAM_WIDTH // ROWS_DEV)
    slot_expert_index = jax.vmap(lambda own, number: assign_block(jax.random.fold_in(splits[4], 2), own, number, ROWS_DEV, EXPERTS, TOPK, CAP, 2))(slot_expert_index_keys, slot_expert_index_turns).reshape((USER_TOTAL, BEAM_WIDTH, TOPK))
    attention_norm_gain = jnp.clip(1.0 + 0.18 * jax.random.normal(splits[5], (D,), jnp.float32), 0.1, 1.9)
    query_projection_weight = centred(splits[6], (D, NH * HD), D ** -0.5, 0.125, ((1, 4),))
    key_projection_weight = centred(splits[7], (D, NH * HD), (D // 12) ** -0.5, 0.4375, ((1, 4),))
    value_projection_weight = centred(splits[8], (D, NH * HD), D ** -0.5, 0.125, ((1, 4),))
    attention_output_weight = centred(splits[9], (NH * HD, D), (NH * HD) ** -0.5, 0.125, ((0, 4),))
    history_event_keys = draw_history_event_keys(jax.random.fold_in(splits[19], 71), 0)
    history_event_values = centred(splits[11], (USER_TOTAL, H, NH * HD), 1.0, 6.0, ((0, 32), (2, 4)))
    decoded_beam_keys = centred(splits[12], (USER_TOTAL, BEAM_WIDTH, STEPS, NH * HD), 3.5, 16.0, ((0, 32), (3, 4)))
    decoded_beam_values = centred(splits[13], (USER_TOTAL, BEAM_WIDTH, STEPS, NH * HD), 1.0, 6.0, ((0, 32), (3, 4)))
    expert_norm_gain = jnp.clip(1.0 + 0.18 * jax.random.normal(splits[14], (D,), jnp.float32), 0.1, 1.9)
    router_projection_weight = centred(splits[15], (D, EXPERTS), D ** -0.5, 0.125)
    expert_gate_weight = centred(splits[16], (EXPERTS, D, EH), D ** -0.5, 0.125, ((0, 32), (2, 4)))
    expert_up_weight = centred(splits[17], (EXPERTS, D, EH), D ** -0.5, 0.125, ((0, 32), (2, 4)))
    expert_down_weight = centred(splits[18], (EXPERTS, EH, D), EH ** -0.5, 0.125, ((0, 32), (1, 4)))
    return {"candidate_hidden_states": candidate_hidden_states, "kept_candidate_index": kept_candidate_index, "slot_parent_beam": slot_parent_beam, "alive_slot_counts": alive_slot_counts, "slot_expert_index": slot_expert_index, "attention_norm_gain": attention_norm_gain, "query_projection_weight": query_projection_weight, "key_projection_weight": key_projection_weight, "value_projection_weight": value_projection_weight, "attention_output_weight": attention_output_weight, "history_event_keys": history_event_keys, "history_event_values": history_event_values, "decoded_beam_keys": decoded_beam_keys, "decoded_beam_values": decoded_beam_values, "expert_norm_gain": expert_norm_gain, "router_projection_weight": router_projection_weight, "expert_gate_weight": expert_gate_weight, "expert_up_weight": expert_up_weight, "expert_down_weight": expert_down_weight}


EPSILON = 1e-05

def rms_scale(values, gain):
    mean_square = lax.optimization_barrier(jnp.mean(values * values, axis=-1, keepdims=True))
    return values * lax.rsqrt(mean_square + EPSILON) * gain

def attend_user(operands):
    query_rows, new_key, new_value, keys_hist, values_hist, past_keys, past_values = operands
    score_scale = HD ** (-0.5)
    query_f = query_rows.astype(jnp.float32)
    keys_f = keys_hist.astype(jnp.float32).reshape(H, NH, HD)
    values_f = values_hist.astype(jnp.float32).reshape(H, NH, HD)
    past_kf = past_keys.astype(jnp.float32).reshape(BEAM_WIDTH, STEPS, NH, HD)
    past_vf = past_values.astype(jnp.float32).reshape(BEAM_WIDTH, STEPS, NH, HD)
    score_hist = jnp.einsum('bhd,khd->bhk', query_f, keys_f) * score_scale
    score_past = jnp.einsum('bhd,bshd->bhs', query_f, past_kf) * score_scale
    score_new = lax.optimization_barrier(jnp.sum(query_f * new_key.astype(jnp.float32), axis=-1)) * score_scale
    highest = jnp.maximum(jnp.maximum(lax.optimization_barrier(jnp.max(score_hist, axis=-1)), lax.optimization_barrier(jnp.max(score_past, axis=-1))), score_new)
    exp_hist = jnp.exp(score_hist - highest[..., None])
    exp_past = jnp.exp(score_past - highest[..., None])
    exp_new = jnp.exp(score_new - highest)
    total_mass = lax.optimization_barrier(jnp.sum(exp_hist, axis=-1)) + lax.optimization_barrier(jnp.sum(exp_past, axis=-1)) + exp_new
    weight_hist = (exp_hist / total_mass[..., None]).astype(jnp.bfloat16)
    weight_past = (exp_past / total_mass[..., None]).astype(jnp.bfloat16)
    weight_new = (exp_new / total_mass).astype(jnp.bfloat16)
    mixed_rows = jnp.einsum('bhk,khd->bhd', weight_hist.astype(jnp.float32), values_f)
    mixed_rows = mixed_rows + jnp.einsum('bhs,bshd->bhd', weight_past.astype(jnp.float32), past_vf)
    mixed_rows = mixed_rows + weight_new.astype(jnp.float32)[..., None] * new_value.astype(jnp.float32)
    return mixed_rows.astype(jnp.bfloat16).reshape(BEAM_WIDTH, NH * HD)

def reference(candidate_hidden_states, kept_candidate_index, slot_parent_beam, alive_slot_counts, slot_expert_index, attention_norm_gain, query_projection_weight, key_projection_weight, value_projection_weight, attention_output_weight, history_event_keys, history_event_values, decoded_beam_keys, decoded_beam_values, expert_norm_gain, router_projection_weight, expert_gate_weight, expert_up_weight, expert_down_weight):
    user_count = candidate_hidden_states.shape[0]
    total_row_count = user_count * BEAM_WIDTH
    decoder_state = jnp.take_along_axis(candidate_hidden_states, kept_candidate_index[:, :, None], axis=1).astype(jnp.float32)
    slot_is_alive = (jnp.arange(BEAM_WIDTH, dtype=jnp.int32)[None, :] < alive_slot_counts[:, None]).reshape(total_row_count)
    past_keys = jnp.take_along_axis(decoded_beam_keys, slot_parent_beam[:, :, None, None], axis=1)
    past_values = jnp.take_along_axis(decoded_beam_values, slot_parent_beam[:, :, None, None], axis=1)
    normed = rms_scale(decoder_state, attention_norm_gain).astype(jnp.bfloat16).reshape(total_row_count, D)
    query_rows = jnp.dot(normed, query_projection_weight, preferred_element_type=jnp.float32).astype(jnp.bfloat16).reshape(user_count, BEAM_WIDTH, NH, HD)
    new_key = jnp.dot(normed, key_projection_weight, preferred_element_type=jnp.float32).astype(jnp.bfloat16).reshape(user_count, BEAM_WIDTH, NH, HD)
    new_value = jnp.dot(normed, value_projection_weight, preferred_element_type=jnp.float32).astype(jnp.bfloat16).reshape(user_count, BEAM_WIDTH, NH, HD)
    attended = lax.map(attend_user, (query_rows, new_key, new_value, history_event_keys, history_event_values, past_keys, past_values))
    resid = decoder_state.reshape(total_row_count, D) + jnp.dot(attended.reshape(total_row_count, NH * HD), attention_output_weight, preferred_element_type=jnp.float32)
    ffn_in = rms_scale(resid, expert_norm_gain).astype(jnp.bfloat16)
    logits = jnp.dot(ffn_in, router_projection_weight, preferred_element_type=jnp.float32)
    choice_ids = slot_expert_index.reshape(total_row_count, TOPK)
    picked = jnp.take_along_axis(logits, choice_ids, axis=1)
    sigmoids = jax.nn.sigmoid(picked)
    gate_values = sigmoids / lax.optimization_barrier(jnp.sum(sigmoids, axis=-1, keepdims=True))
    pair_expert = choice_ids.reshape(-1)
    pair_live = jnp.repeat(slot_is_alive, TOPK)
    pair_row = jnp.arange(total_row_count * TOPK, dtype=jnp.int32) // TOPK
    slots_max = N_DP * CAP

    def run_expert(operands):
        expert_index, gate_w, up_w, down_w = operands
        mine = (pair_expert == expert_index) & pair_live
        order_rows = jnp.argsort(jnp.where(mine, 0, 1).astype(jnp.int32), stable=True)[:slots_max].astype(jnp.int32)
        valid_slots = mine[order_rows]
        taken_rows = ffn_in[pair_row[order_rows]]
        activated = jax.nn.silu(jnp.dot(taken_rows, gate_w, preferred_element_type=jnp.float32)) * jnp.dot(taken_rows, up_w, preferred_element_type=jnp.float32)
        activated = activated.astype(jnp.bfloat16)
        result = jnp.dot(activated, down_w, preferred_element_type=jnp.float32) * valid_slots[:, None].astype(jnp.float32)
        return (result, order_rows)
    results, orders = lax.map(run_expert, (jnp.arange(EXPERTS, dtype=jnp.int32), expert_gate_weight, expert_up_weight, expert_down_weight))
    per_pair = jnp.zeros((total_row_count * TOPK, D), jnp.float32).at[orders.reshape(-1)].add(results.reshape(-1, D))
    mixed_rows = lax.optimization_barrier(jnp.sum(gate_values[:, :, None] * per_pair.reshape(total_row_count, TOPK, D), axis=1))
    output = jnp.where(slot_is_alive[:, None], resid + mixed_rows, 0.0).astype(jnp.bfloat16)
    return output.reshape(user_count, BEAM_WIDTH, D)
```

```python
import functools
import math

import jax
import jax.numpy as jnp
from jax import lax
from jax.experimental import pallas as pl
from jax.experimental.pallas import tpu as pltpu
from jax.sharding import PartitionSpec as P

HD = 128
EPSILON = 1e-05
BF16 = jnp.bfloat16
F32 = jnp.float32
MIB = 1024 * 1024
WHOLE = pl.BlockSpec(memory_space=pltpu.VMEM)
IN_HBM = pl.BlockSpec(memory_space=pl.ANY)
IN_SMEM = pl.BlockSpec(memory_space=pltpu.SMEM)


def mm(a, b):
    return jnp.dot(a, b, preferred_element_type=F32)


def mm_nt(a, b):
    return lax.dot_general(a, b, (((1,), (1,)), ((), ())), preferred_element_type=F32)


def iota(shape, dim):
    return lax.broadcasted_iota(jnp.int32, shape, dim)


def call(kernel, out, in_specs, vmem_mib, flops, nbytes, scratch=(), transcendentals=0):
    return pl.pallas_call(
        kernel,
        out_shape=out,
        in_specs=in_specs,
        out_specs=jax.tree.map(lambda _: WHOLE, out),
        scratch_shapes=list(scratch),
        compiler_params=pltpu.CompilerParams(vmem_limit_bytes=vmem_mib * MIB),
        cost_estimate=pl.CostEstimate(
            flops=flops, bytes_accessed=nbytes, transcendentals=transcendentals
        ),
    )


def attention_kernel(
    kept, parent, gain, state_h, wq_h, wk_h, wv_h, wo_h, kh_h, vh_h, dk_h, dv_h,
    keep_own, keep_other, send,
    st, wq, wk, wv, wo, kh, vh, dk, dv, x, nrm, q, k, v, att, sems,
):
    users, slots, width = st.shape
    feat = wq.shape[1]
    heads = feat // HD
    sec = lax.axis_index("sec")
    z, c = sec // 2, sec % 2
    moves = {}

    def start(name, src, dst):
        copy = pltpu.make_async_copy(src, dst, sems.at[len(moves)])
        copy.start()
        moves[name] = copy

    start("st", state_h, st)
    start("wq", wq_h, wq)
    start("wk", wk_h, wk)
    start("wv", wv_h, wv)
    start("dk", dk_h, dk)
    start("dv", dv_h, dv)
    for u in range(users):
        start(("kh", u), kh_h.at[u], kh.at[u])
        start(("vh", u), vh_h.at[u], vh.at[u])
    start("wo", wo_h, wo)

    moves["st"].wait()
    for u in range(users):
        rows = pl.ds(u * slots, slots)
        pick = (iota((slots, slots), 0) == kept[u : u + 1, :]).astype(F32).T.astype(BF16)
        xu = mm(pick, st[u])
        x[rows, :] = xu
        mean = jnp.mean(xu * xu, axis=-1, keepdims=True)
        nrm[rows, :] = (xu * lax.rsqrt(mean + EPSILON) * gain[...]).astype(BF16)
    moves["wq"].wait()
    q[...] = mm(nrm[...], wq[...]).astype(BF16)
    moves["wk"].wait()
    k[...] = mm(nrm[...], wk[...]).astype(BF16)
    moves["wv"].wait()
    v[...] = mm(nrm[...], wv[...]).astype(BF16)
    moves["dk"].wait()
    moves["dv"].wait()

    scale = HD ** (-0.5) * math.log2(math.e)
    steps = dk.shape[1] // slots
    for u in range(users):
        rows = pl.ds(u * slots, slots)
        pk, pv = [], []
        for s in range(steps):
            hot = iota((steps * slots, slots), 0) == parent[u : u + 1, :] * steps + s
            pick = hot.astype(F32).T.astype(BF16)
            pk.append(mm(pick, dk[u]))
            pv.append(mm(pick, dv[u]))
        moves[("kh", u)].wait()
        moves[("vh", u)].wait()
        for h in range(heads):
            cols = slice(h * HD, (h + 1) * HD)
            qh = q[rows, cols]
            qf = qh.astype(F32)
            s_hist = mm_nt(qh, kh[u, :, cols])
            s_more = [jnp.sum(qf * p[:, cols], axis=-1, keepdims=True) for p in pk]
            s_more.append(jnp.sum(qf * k[rows, cols].astype(F32), axis=-1, keepdims=True))
            top = jnp.max(s_hist, axis=-1, keepdims=True)
            for s in s_more:
                top = jnp.maximum(top, s)
            e_hist = jnp.exp2((s_hist - top) * scale)
            mass = jnp.sum(e_hist, axis=-1, keepdims=True)
            mixed = mm(e_hist.astype(BF16), vh[u, :, cols])
            values = [p[:, cols] for p in pv] + [v[rows, cols].astype(F32)]
            for s, value in zip(s_more, values):
                e = jnp.exp2((s - top) * scale)
                mass = mass + e
                mixed = mixed + e * value
            att[rows, cols] = (mixed / mass).astype(BF16)

    moves["wo"].wait()

    def project(quarter):
        return mm(att[...], wo[:, pl.ds(pl.multiple_of(quarter * feat, feat), feat)])

    send[:, :feat] = project(2 * z + 1 - c).astype(BF16)
    send[:, feat:] = project(2 * (1 - z) + 1 - c).astype(BF16)
    keep_other[...] = project(2 * (1 - z) + c)
    keep_own[...] = project(sec) + x[:, pl.ds(pl.multiple_of(sec * feat, feat), feat)]


def routing_kernel(alive, choice, place, where):
    users, top, slots = choice.shape
    rows = users * slots
    lane = iota((1, slots), 1)
    live = jnp.concatenate([lane < alive[u] for u in range(users)], axis=1)
    experts = place.shape[0] // (6 * 8)
    earlier = (iota((rows, rows), 0) < iota((rows, rows), 1)).astype(F32).astype(BF16)
    base = jnp.zeros((experts, 1), F32)
    main, extra = [], []
    for t in range(top):
        e = jnp.concatenate([choice[u, t : t + 1, :] for u in range(users)], axis=1)
        hot = ((iota((experts, rows), 0) == e) & live).astype(F32)
        before = mm(hot.astype(BF16), earlier)
        rank = jnp.sum(hot * (before + base), axis=0, keepdims=True).astype(jnp.int32)
        base = base + jnp.sum(hot, axis=1, keepdims=True)
        over = rank - 16
        main.append(
            jnp.where(live & (rank < 16), (rank >> 3) * (experts * 8) + e * 8 + (rank & 7), -1)
        )
        extra.append(
            jnp.where(live & (rank >= 16), (over >> 2) * (experts * 8) + e * 8 + (over & 3), -8)
        )
    span = 2 * experts * 8
    index = iota((span, rows), 0)
    for part, (a, b) in enumerate(
        ((main[0], main[1]), (extra[0], extra[1]), (extra[0] + 4, extra[1] + 4))
    ):
        hit = (index == a) | (index == b)
        place[part * span : (part + 1) * span, :] = hit.astype(F32).astype(BF16)
    blank = jnp.zeros((4, rows), jnp.int32)
    where[...] = jnp.concatenate(main + extra + [blank], axis=0)


def dispatch_kernel(keep, from_core, from_z, gain, place, resid, message):
    feat = keep.shape[1]
    half = feat // 2
    span = place.shape[0] // 3
    sec = lax.axis_index("sec")
    r = keep[...] + from_core[:, :feat].astype(F32) + from_z[...].astype(F32)
    resid[...] = r
    scaled = (r * gain[:, pl.ds(pl.multiple_of(sec * feat, feat), feat)]).astype(BF16)
    main = mm(place[:span, :], scaled).astype(BF16)
    folded = mm(place[span : 2 * span, :], scaled[:, :half])
    folded = (folded + mm(place[2 * span :, :], scaled[:, half:])).astype(BF16)
    for z in range(2):
        message[z * span : (z + 1) * span, :feat] = main
        message[z * span : (z + 1) * span, feat:] = folded


def router_kernel(resid, gain, router, choice, part):
    users, top, slots = choice.shape
    rows = users * slots
    feat = resid.shape[1]
    experts = router.shape[0]
    sec = lax.axis_index("sec")
    cols = pl.ds(pl.multiple_of(sec * feat, feat), feat)
    r = resid[...]
    scaled = (r * gain[:, cols]).astype(BF16)
    logits = mm_nt(router[:, cols], scaled)
    out = []
    for t in range(top):
        e = jnp.concatenate([choice[u, t : t + 1, :] for u in range(users)], axis=1)
        hot = (iota((experts, rows), 0) == e).astype(F32)
        out.append(jnp.sum(hot * logits, axis=0, keepdims=True))
    squares = lax.dot_general(
        jnp.ones((8, feat), F32), r * r, (((1,), (1,)), ((), ())),
        precision=lax.Precision.HIGHEST, preferred_element_type=F32,
    )
    part[...] = jnp.concatenate(out + [squares[: 8 - top]], axis=0)


def gate_kernel(p0, p1, p2, p3, where, gates):
    rows = where.shape[1]
    total = (p0[...] + p1[...]) + (p2[...] + p3[...])
    width = gates.shape[1] // 3 * 4
    scale = lax.rsqrt(total[2:3] / width + EPSILON)
    sig = [1.0 / (1.0 + jnp.exp(-(total[t : t + 1] * scale))) for t in range(2)]
    weight = [s / (sig[0] + sig[1]) for s in sig]
    span = gates.shape[1] // 3
    index = iota((span, rows), 0)
    for part, shift in enumerate((0, 0, 4)):
        first = 0 if part == 0 else 2
        g = jnp.where(index == where[first : first + 1, :] + shift, weight[0], 0.0)
        g = jnp.where(index == where[first + 1 : first + 2, :] + shift, weight[1], g)
        gates[:, part * span : (part + 1) * span] = g.T.astype(BF16)


def fold_matrices(count):
    slot, place = iota((count * 4, count * 8), 0), iota((count * 4, count * 8), 1)
    at = (slot // 4) * 8 + slot % 4
    return [(place == at + shift).astype(F32) for shift in (0, 4)]


def expert_kernel(
    arrived, gain, wg0_h, wu0_h, wd0_h, wg1_h, wu1_h, wd1_h, message,
    wg0, wu0, wd0, wg1, wu1, wd1, x, act, sems,
):
    width, hidden = wg0.shape
    quarters = 4
    feat = width // quarters
    half = feat // 2
    block = arrived.shape[0] // quarters
    sources = block // 8
    copies = []
    for n, (src, dst) in enumerate(
        ((wg0_h, wg0), (wu0_h, wu0), (wg1_h, wg1), (wu1_h, wu1), (wd0_h, wd0), (wd1_h, wd1))
    ):
        copies.append(pltpu.make_async_copy(src.at[0], dst, sems.at[n]))
        copies[-1].start()
    folds = fold_matrices(sources)
    unfold = [f.astype(BF16) for f in folds]
    refold = [f.T.astype(BF16) for f in folds]
    for p in range(quarters):
        rows = slice(p * block, (p + 1) * block)
        x[:block, p * feat : (p + 1) * feat] = arrived[rows, :feat]
        tail = arrived[rows, feat:]
        for n in range(2):
            at = p * feat + n * half
            x[block:, at : at + half] = mm(unfold[n], tail).astype(BF16)
    plain = x[...].astype(F32) * (1.0 / gain[...])
    scale = lax.rsqrt(jnp.mean(plain * plain, axis=-1, keepdims=True) + EPSILON)
    for n, (wg, wu) in enumerate(((wg0, wu0), (wg1, wu1))):
        copies[2 * n].wait()
        g = mm(x[...], wg[...]) * scale
        copies[2 * n + 1].wait()
        u = mm(x[...], wu[...]) * scale
        act[:, n * hidden : (n + 1) * hidden] = (g / (1.0 + jnp.exp(-g)) * u).astype(BF16)
    copies[4].wait()
    copies[5].wait()
    for p in range(quarters):
        cols = slice(p * feat, (p + 1) * feat)
        rows = slice(p * block, (p + 1) * block)
        y = mm(act[:, :hidden], wd0[:, cols]) + mm(act[:, hidden:], wd1[:, cols])
        y = y.astype(BF16)
        message[rows, :feat] = y[:block]
        tail = mm(refold[0], y[block:, :half]) + mm(refold[1], y[block:, half:])
        message[rows, feat:] = tail.astype(BF16)


def combine_kernel(alive, resid, gates, arrived, out):
    users, slots, feat = out.shape
    half = feat // 2
    span = gates.shape[1] // 3
    main = jnp.zeros((users * slots, feat), F32)
    left = jnp.zeros((users * slots, half), F32)
    right = left
    for z in range(2):
        rows = slice(z * span, (z + 1) * span)
        tail = arrived[rows, feat:]
        main = main + mm(gates[:, :span], arrived[rows, :feat])
        left = left + mm(gates[:, span : 2 * span], tail)
        right = right + mm(gates[:, 2 * span :], tail)
    total = resid[...] + main + jnp.concatenate([left, right], axis=1)
    for u in range(users):
        live = iota((slots, feat), 0) < alive[u]
        rows = slice(u * slots, (u + 1) * slots)
        out[u] = jnp.where(live, total[rows], 0.0).astype(BF16)


def on_device(
    candidate_hidden_states,
    kept_candidate_index,
    slot_parent_beam,
    alive_slot_counts,
    slot_expert_index,
    attention_norm_gain,
    query_projection_weight,
    key_projection_weight,
    value_projection_weight,
    attention_output_weight,
    history_event_keys,
    history_event_values,
    decoded_beam_keys,
    decoded_beam_values,
    expert_norm_gain,
    router_projection_weight,
    expert_gate_weight,
    expert_up_weight,
    expert_down_weight,
):
    users, slots, width = candidate_hidden_states.shape
    feat = query_projection_weight.shape[1]
    history = history_event_keys.shape[1]
    steps = decoded_beam_keys.shape[2]
    experts = router_projection_weight.shape[1]
    hidden = expert_gate_weight.shape[2]
    rows = users * slots
    span = 2 * experts * 8
    core = [(s, s ^ 1) for s in range(4)]
    z_far = [(s, s ^ 2) for s in range(4)]
    both = [(s, s ^ 3) for s in range(4)]
    everyone = ("sec", "dp")
    struct = jax.ShapeDtypeStruct

    attention_gain = attention_norm_gain.reshape(1, width)
    expert_gain = expert_norm_gain.reshape(1, width)
    choice = jnp.swapaxes(slot_expert_index, 1, 2)
    router = router_projection_weight.T
    past_keys = decoded_beam_keys.reshape(users, slots * steps, feat)
    past_values = decoded_beam_values.reshape(users, slots * steps, feat)

    with jax.named_scope("attention"):
        keep_own, keep_other, send = call(
            attention_kernel,
            (struct((rows, feat), F32), struct((rows, feat), F32), struct((rows, 2 * feat), BF16)),
            [WHOLE] * 3 + [IN_HBM] * 9,
            50,
            3_300_000_000,
            20_000_000,
            [
                pltpu.VMEM((users, slots, width), BF16),
                pltpu.VMEM((width, feat), BF16),
                pltpu.VMEM((width, feat), BF16),
                pltpu.VMEM((width, feat), BF16),
                pltpu.VMEM((feat, width), BF16),
                pltpu.VMEM((users, history, feat), BF16),
                pltpu.VMEM((users, history, feat), BF16),
                pltpu.VMEM((users, slots * steps, feat), BF16),
                pltpu.VMEM((users, slots * steps, feat), BF16),
                pltpu.VMEM((rows, width), F32),
                pltpu.VMEM((rows, width), BF16),
                pltpu.VMEM((rows, feat), BF16),
                pltpu.VMEM((rows, feat), BF16),
                pltpu.VMEM((rows, feat), BF16),
                pltpu.VMEM((rows, feat), BF16),
                pltpu.SemaphoreType.DMA((7 + 2 * users,)),
            ],
            2_200_000,
        )(
            kept_candidate_index, slot_parent_beam, attention_gain, candidate_hidden_states,
            query_projection_weight, key_projection_weight, value_projection_weight,
            attention_output_weight, history_event_keys, history_event_values,
            past_keys, past_values,
        )
    with jax.named_scope("sibling_weights"):
        weights = [expert_gate_weight, expert_up_weight, expert_down_weight]
        sibling = [lax.ppermute(w, "sec", core) for w in weights]
    with jax.named_scope("head_sum"):
        from_core = lax.ppermute(send, "sec", core)
        to_z = (keep_other + from_core[:, feat:].astype(F32)).astype(BF16)
        from_z = lax.ppermute(to_z, "sec", z_far)
    with jax.named_scope("routing"):
        place, where = call(
            routing_kernel,
            (struct((3 * span, rows), BF16), struct((8, rows), jnp.int32)),
            [IN_SMEM, WHOLE],
            16,
            10_000_000,
            1_000_000,
        )(alive_slot_counts, choice)
    with jax.named_scope("dispatch"):
        resid, message = call(
            dispatch_kernel,
            (struct((rows, feat), F32), struct((2 * span, feat * 3 // 2), BF16)),
            [WHOLE] * 5,
            24,
            300_000_000,
            4_000_000,
        )(keep_own, from_core, from_z, expert_gain, place)
        arrived = lax.all_to_all(message, everyone, 0, 0, tiled=True)
    with jax.named_scope("router"):
        part = call(
            router_kernel,
            struct((8, rows), F32),
            [WHOLE] * 4,
            16,
            30_000_000,
            1_000_000,
        )(resid, expert_gain, router, choice)
        parts = [lax.ppermute(part, "sec", pairs) for pairs in (core, z_far, both)]
    with jax.named_scope("gates"):
        gates = call(
            gate_kernel,
            struct((rows, 3 * span), BF16),
            [WHOLE] * 5,
            16,
            3_000_000,
            1_000_000,
        )(part, *parts, where)
    with jax.named_scope("experts"):
        result = call(
            expert_kernel,
            struct((2 * span, feat * 3 // 2), BF16),
            [WHOLE] * 2 + [IN_HBM] * 6,
            50,
            4_800_000_000,
            16_000_000,
            [
                pltpu.VMEM((width, hidden), BF16),
                pltpu.VMEM((width, hidden), BF16),
                pltpu.VMEM((hidden, width), BF16),
                pltpu.VMEM((width, hidden), BF16),
                pltpu.VMEM((width, hidden), BF16),
                pltpu.VMEM((hidden, width), BF16),
                pltpu.VMEM((experts * 12, width), BF16),
                pltpu.VMEM((experts * 12, 2 * hidden), BF16),
                pltpu.SemaphoreType.DMA((6,)),
            ],
            400_000,
        )(arrived, expert_gain, *weights, *sibling)
        returned = lax.all_to_all(result, everyone, 0, 0, tiled=True)
    with jax.named_scope("combine"):
        return call(
            combine_kernel,
            struct((users, slots, feat), BF16),
            [IN_SMEM] + [WHOLE] * 3,
            24,
            600_000_000,
            4_000_000,
        )(alive_slot_counts, resid, gates, returned)


def solution(mesh):
    in_specs = (
        P("dp", None, None),
        P("dp", None),
        P("dp", None),
        P("dp"),
        P("dp", None, None),
        P(),
        P(None, "sec"),
        P(None, "sec"),
        P(None, "sec"),
        P("sec", None),
        P("dp", None, "sec"),
        P("dp", None, "sec"),
        P("dp", None, None, "sec"),
        P("dp", None, None, "sec"),
        P(),
        P(),
        P("dp", None, "sec"),
        P("dp", None, "sec"),
        P("dp", "sec", None),
    )
    out_specs = P("dp", None, "sec")
    return jax.shard_map(
        on_device, mesh=mesh, in_specs=in_specs, out_specs=out_specs, check_vma=False
    )
```

```python
import functools
import math

import jax
import jax.numpy as jnp
from jax import lax
from jax.experimental import pallas as pl
from jax.experimental.pallas import tpu as pltpu
from jax.sharding import PartitionSpec as P

HD = 128
EPSILON = 1e-05
BF16 = jnp.bfloat16
F32 = jnp.float32
MIB = 1024 * 1024
WHOLE = pl.BlockSpec(memory_space=pltpu.VMEM)
IN_HBM = pl.BlockSpec(memory_space=pl.ANY)
IN_SMEM = pl.BlockSpec(memory_space=pltpu.SMEM)


def mm(a, b):
    return jnp.dot(a, b, preferred_element_type=F32)


def mm_nt(a, b):
    return lax.dot_general(a, b, (((1,), (1,)), ((), ())), preferred_element_type=F32)


def iota(shape, dim):
    return lax.broadcasted_iota(jnp.int32, shape, dim)


def call(kernel, out, in_specs, vmem_mib, flops, nbytes, scratch=(), transcendentals=0, out_specs=None):
    return pl.pallas_call(
        kernel,
        out_shape=out,
        in_specs=in_specs,
        out_specs=jax.tree.map(lambda _: WHOLE, out) if out_specs is None else out_specs,
        scratch_shapes=list(scratch),
        compiler_params=pltpu.CompilerParams(vmem_limit_bytes=vmem_mib * MIB),
        cost_estimate=pl.CostEstimate(
            flops=flops, bytes_accessed=nbytes, transcendentals=transcendentals
        ),
    )


class Loads:
    def __init__(self, sems):
        self.sems = sems
        self.copies, self.count = {}, 0

    def start(self, name, *pieces):
        for src, dst in pieces:
            copy = pltpu.make_async_copy(src, dst, self.sems.at[self.count])
            copy.start()
            self.copies.setdefault(name, []).append(copy)
            self.count += 1

    def start_rows(self, name, src, dst, pieces):
        size = dst.shape[0] // pieces
        cuts = [pl.ds(n * size, size) for n in range(pieces)]
        self.start(name, *[(src.at[cut], dst.at[cut]) for cut in cuts])

    def wait(self, name):
        for copy in self.copies[name]:
            copy.wait()


def attention_kernel(
    kept_h, parent_h, gain_h, state_h, wq_h, wk_h, wv_h, wo_h, kh_h, vh_h, dk_h, dv_h,
    keep_own, keep_other, send,
    kept, parent, gain, st, sq, wq, wk, wv, wo, kh, vh, dk, dv, nrm, q, k, v, own, att, scores, sems,
):
    users, slots, width = st.shape
    history = kh.shape[1]
    feat = wq.shape[1]
    heads = feat // HD
    sec = lax.axis_index("sec")
    z, c = sec // 2, sec % 2

    def quarter(n):
        return pl.ds(pl.multiple_of(n * feat, feat), feat)

    order = (sec, 2 * (1 - z) + c, 2 * z + 1 - c, 2 * (1 - z) + 1 - c)
    loads = Loads(sems)
    loads.start("small", (kept_h, kept), (parent_h, parent), (gain_h, gain))
    for u in range(users):
        loads.start_rows(("st", u), state_h.at[u], st.at[u], 2)
    loads.start_rows("wq", wq_h, wq, 4)
    loads.start_rows("wk", wk_h, wk, 4)
    loads.start_rows("wv", wv_h, wv, 4)
    for u in range(users):
        loads.start(
            ("past", u),
            (dk_h.at[u].reshape(dk.shape[1:]), dk.at[u]),
            (dv_h.at[u].reshape(dv.shape[1:]), dv.at[u]),
        )
        loads.start_rows(("kh", u), kh_h.at[u], kh.at[u], 4)
        loads.start_rows(("vh", u), vh_h.at[u], vh.at[u], 4)
    loads.start("sq", (state_h.at[:, :, quarter(sec)], sq))
    loads.start("wo", *[
        (wo_h.at[:, quarter(n)], wo.at[:, pl.ds(at * feat, feat)]) for at, n in enumerate(order)
    ])

    loads.wait("small")
    picks = []
    for u in range(users):
        rows = pl.ds(u * slots, slots)
        picks.append((iota((slots, slots), 0) == kept[u : u + 1, :]).astype(F32).T.astype(BF16))
        loads.wait(("st", u))
        xu = mm(picks[u], st[u])
        mean = jnp.mean(xu * xu, axis=-1, keepdims=True)
        nrm[rows, :] = (xu * lax.rsqrt(mean + EPSILON) * gain[...]).astype(BF16)
    loads.wait("wq")
    q[...] = mm(nrm[...], wq[...]).astype(BF16)
    loads.wait("wk")
    k[...] = mm(nrm[...], wk[...]).astype(BF16)
    loads.wait("wv")
    v[...] = mm(nrm[...], wv[...]).astype(BF16)

    scale = HD ** (-0.5) * math.log2(math.e)
    steps = dk.shape[1] // slots
    chunk = 512
    chunks = [slice(a, a + chunk) for a in range(0, history, chunk)]
    group = 2
    tall, wide = group * slots, group * HD
    sets = [(u, h) for u in range(users) for h in range(0, heads, group)]
    past = {}
    ready = {}

    def stack(f):
        return jnp.concatenate([f(slice(m * HD, (m + 1) * HD)) for m in range(group)], axis=0)

    for n in range(len(sets) + 1):
        if n < len(sets):
            u, h = sets[n]
            rows = pl.ds(u * slots, slots)
            cols = slice(h * HD, h * HD + wide)
            if h == 0:
                loads.wait(("past", u))
                past[u] = []
                for s in range(steps):
                    hot = iota((steps * slots, slots), 0) == parent[u : u + 1, :] * steps + s
                    pick = hot.astype(F32).T.astype(BF16)
                    past[u].append((mm(pick, dk[u]), mm(pick, dv[u])))
                loads.wait(("kh", u))
                loads.wait(("vh", u))
            qs = q[rows, cols]
            blank = jnp.zeros((slots, HD), BF16)
            diagonal = jnp.concatenate(
                [
                    jnp.concatenate(
                        [qs[:, m * HD : (m + 1) * HD] if m == at else blank for m in range(group)], axis=1
                    )
                    for at in range(group)
                ],
                axis=0,
            )
            qf = qs.astype(F32)
            more = []
            for p in [p for p, _ in past[u]] + [k[rows, :].astype(F32)]:
                both = qf * p[:, cols]
                more.append(stack(lambda m: jnp.sum(both[:, m], axis=-1, keepdims=True)))
            high = jnp.full((tall, HD), -jnp.inf, F32)
        if n > 0:
            u0, h0, more0, top = ready.pop(n - 1)
            rows0 = pl.ds(u0 * slots, slots)
            cols0 = slice(h0 * HD, h0 * HD + wide)
            mass = jnp.zeros((tall, HD), F32)
            mixed = jnp.zeros((tall, wide), F32)
        for at in chunks:
            if n < len(sets):
                s = mm_nt(diagonal, kh[u, at, cols])
                scores[n % 2, :, at] = s
                for a in range(0, chunk, HD):
                    high = jnp.maximum(high, s[:, a : a + HD])
            if n > 0:
                e = jnp.exp2((scores[(n - 1) % 2, :, at] - top) * scale)
                for a in range(0, chunk, HD):
                    mass = mass + e[:, a : a + HD]
                mixed = mixed + mm(e.astype(BF16), vh[u0, at, cols0])
        if n < len(sets):
            peak = jnp.max(high, axis=-1, keepdims=True)
            for s in more:
                peak = jnp.maximum(peak, s)
            ready[n] = (u, h, more, peak)
        if n > 0:
            total = jnp.sum(mass, axis=-1, keepdims=True)
            mixed = jnp.concatenate(
                [mixed[m * slots : (m + 1) * slots, m * HD : (m + 1) * HD] for m in range(group)], axis=0
            )
            values = [p[:, cols0] for _, p in past[u0]] + [v[rows0, cols0].astype(F32)]
            for s, value in zip(more0, values):
                e = jnp.exp2((s - top) * scale)
                total = total + e
                mixed = mixed + e * stack(lambda m: value[:, m])
            mixed = (mixed / total).astype(BF16)
            att[rows0, cols0] = jnp.concatenate(
                [mixed[m * slots : (m + 1) * slots] for m in range(group)], axis=1
            )

    loads.wait("sq")
    for u in range(users):
        own[pl.ds(u * slots, slots), :] = mm(picks[u], sq[u]).astype(BF16)
    loads.wait("wo")
    out = mm(att[...], wo[...])
    keep_own[...] = out[:, :feat] + own[...].astype(F32)
    keep_other[...] = out[:, feat : 2 * feat]
    send[...] = out[:, 2 * feat :].astype(BF16)


def routing_kernel(alive, choice, place, where):
    users, top, slots = choice.shape
    rows = users * slots
    lane = iota((1, slots), 1)
    live = jnp.concatenate([lane < alive[u] for u in range(users)], axis=1)
    experts = place.shape[0] // (6 * 8)
    earlier = (iota((rows, rows), 0) < iota((rows, rows), 1)).astype(F32).astype(BF16)
    base = jnp.zeros((experts, 1), F32)
    main, extra = [], []
    for t in range(top):
        e = jnp.concatenate([choice[u, t : t + 1, :] for u in range(users)], axis=1)
        hot = ((iota((experts, rows), 0) == e) & live).astype(F32)
        before = mm(hot.astype(BF16), earlier)
        rank = jnp.sum(hot * (before + base), axis=0, keepdims=True).astype(jnp.int32)
        base = base + jnp.sum(hot, axis=1, keepdims=True)
        over = rank - 16
        main.append(
            jnp.where(live & (rank < 16), (rank >> 3) * (experts * 8) + e * 8 + (rank & 7), -1)
        )
        extra.append(
            jnp.where(live & (rank >= 16), (over >> 2) * (experts * 8) + e * 8 + (over & 3), -8)
        )
    span = 2 * experts * 8
    index = iota((span, rows), 0)
    for part, (a, b) in enumerate(
        ((main[0], main[1]), (extra[0], extra[1]), (extra[0] + 4, extra[1] + 4))
    ):
        hit = (index == a) | (index == b)
        place[part * span : (part + 1) * span, :] = hit.astype(F32).astype(BF16)
    blank = jnp.zeros((4, rows), jnp.int32)
    where[...] = jnp.concatenate(main + extra + [blank], axis=0)


def dispatch_kernel(keep, from_core, from_z, gain, place, resid, message, block, sems):
    feat = keep.shape[1]
    half = feat // 2
    span = place.shape[0] // 3
    part = span // 2
    sec = lax.axis_index("sec")
    r = keep[...] + from_core[:, :feat].astype(F32) + from_z[...].astype(F32)
    scaled = (r * gain[:, pl.ds(pl.multiple_of(sec * feat, feat), feat)]).astype(BF16)
    copies = []
    for n in range(2):
        rows = slice(n * part, (n + 1) * part)
        block[rows, :feat] = mm(place[rows, :], scaled).astype(BF16)
        folded = mm(place[span + n * part : span + (n + 1) * part, :], scaled[:, :half])
        folded = folded + mm(
            place[2 * span + n * part : 2 * span + (n + 1) * part, :], scaled[:, half:]
        )
        block[rows, feat:] = folded.astype(BF16)
        for z in range(2):
            copies.append(
                pltpu.make_async_copy(
                    block.at[pl.ds(n * part, part)],
                    message.at[pl.ds(z * span + n * part, part)],
                    sems.at[len(copies)],
                )
            )
            copies[-1].start()
    resid[...] = r
    for copy in copies:
        copy.wait()


def router_kernel(resid, gain, router, choice, part):
    users, top, slots = choice.shape
    rows = users * slots
    feat = resid.shape[1]
    experts = router.shape[0]
    sec = lax.axis_index("sec")
    cols = pl.ds(pl.multiple_of(sec * feat, feat), feat)
    r = resid[...]
    scaled = (r * gain[:, cols]).astype(BF16)
    logits = mm_nt(router[:, cols], scaled)
    out = []
    for t in range(top):
        e = jnp.concatenate([choice[u, t : t + 1, :] for u in range(users)], axis=1)
        hot = (iota((experts, rows), 0) == e).astype(F32)
        out.append(jnp.sum(hot * logits, axis=0, keepdims=True))
    squares = lax.dot_general(
        jnp.ones((8, feat), F32), r * r, (((1,), (1,)), ((), ())),
        precision=lax.Precision.HIGHEST, preferred_element_type=F32,
    )
    part[...] = jnp.concatenate(out + [squares[: 8 - top]], axis=0)


def gate_kernel(p0, p1, p2, p3, where, gates):
    rows = where.shape[1]
    total = (p0[...] + p1[...]) + (p2[...] + p3[...])
    width = gates.shape[1] // 3 * 4
    scale = lax.rsqrt(total[2:3] / width + EPSILON)
    sig = [1.0 / (1.0 + jnp.exp(-(total[t : t + 1] * scale))) for t in range(2)]
    weight = [s / (sig[0] + sig[1]) for s in sig]
    span = gates.shape[1] // 3
    index = iota((span, rows), 0)
    for part, shift in enumerate((0, 0, 4)):
        first = 0 if part == 0 else 2
        g = jnp.where(index == where[first : first + 1, :] + shift, weight[0], 0.0)
        g = jnp.where(index == where[first + 1 : first + 2, :] + shift, weight[1], g)
        gates[:, part * span : (part + 1) * span] = g.T.astype(BF16)


def unfold(folded):
    rows, width = folded.shape
    pair = folded.astype(F32).reshape(rows // 16, 2, 8, width)
    a, b = pair[:, 0], pair[:, 1]
    first = iota(a.shape, 1) < 4
    left = jnp.where(first, a, pltpu.roll(b, 4, 1))
    right = jnp.where(first, pltpu.roll(a, 4, 1), b)
    return [t.reshape(rows // 2, width).astype(BF16) for t in (left, right)]


def fold(left, right):
    rows, width = left.shape
    left, right = (t.reshape(rows // 8, 8, width) for t in (left, right))
    first = iota(left.shape, 1) < 4
    a = jnp.where(first, left, pltpu.roll(right, 4, 1))
    b = jnp.where(first, pltpu.roll(left, 4, 1), right)
    return jnp.stack([a, b], axis=1).reshape(rows * 2, width)


def expert_kernel(
    arrived, gain, wg0_h, wu0_h, wd0_h, wg1_h, wu1_h, wd1_h, message,
    wg0, wu0, wg1, wu1, wd, x, act, block, sems, out_sems,
):
    width, hidden = wg0.shape
    quarters = 4
    feat = width // quarters
    half = feat // 2
    part = arrived.shape[0] // quarters
    loads = Loads(sems)
    for n, (src, dst) in enumerate(((wg0_h, wg0), (wu0_h, wu0), (wg1_h, wg1), (wu1_h, wu1))):
        loads.start_rows(n, src.at[0], dst, 4)
    loads.start_rows(4, wd0_h.at[0], wd.at[pl.ds(0, hidden)], 4)
    loads.start_rows(5, wd1_h.at[0], wd.at[pl.ds(hidden, hidden)], 4)
    for p in range(quarters):
        rows = slice(p * part, (p + 1) * part)
        x[:part, p * feat : (p + 1) * feat] = arrived[rows, :feat]
        for n, piece in enumerate(unfold(arrived[rows, feat:])):
            at = p * feat + n * half
            x[part:, at : at + half] = piece
    plain = x[...].astype(F32) * (1.0 / gain[...])
    scale = lax.rsqrt(jnp.mean(plain * plain, axis=-1, keepdims=True) + EPSILON)
    for n, (wg, wu) in enumerate(((wg0, wu0), (wg1, wu1))):
        loads.wait(2 * n)
        g = mm(x[...], wg[...]) * scale
        loads.wait(2 * n + 1)
        u = mm(x[...], wu[...]) * scale
        act[:, n * hidden : (n + 1) * hidden] = (g / (1.0 + jnp.exp(-g)) * u).astype(BF16)
    loads.wait(4)
    loads.wait(5)
    copies = []
    for p in range(quarters):
        cols = slice(p * feat, (p + 1) * feat)
        rows = slice(p * part, (p + 1) * part)
        y = mm(act[...], wd[:, cols])
        block[rows, :feat] = y[:part].astype(BF16)
        block[rows, feat:] = fold(y[part:, :half], y[part:, half:]).astype(BF16)
        for n in range(4):
            here = pl.ds(p * part + n * (part // 4), part // 4)
            copies.append(
                pltpu.make_async_copy(block.at[here], message.at[here], out_sems.at[len(copies)])
            )
            copies[-1].start()
    for copy in copies:
        copy.wait()


def combine_kernel(alive, resid, gates, arrived, out):
    users, slots, feat = out.shape
    span = gates.shape[1] // 3

    def bring(part, cols):
        g = gates[:, part * span : (part + 1) * span]
        return mm(jnp.concatenate([g, g], axis=1), arrived[:, cols])

    main = bring(0, slice(0, feat))
    tail = slice(feat, arrived.shape[1])
    total = resid[...] + main + jnp.concatenate([bring(1, tail), bring(2, tail)], axis=1)
    for u in range(users):
        live = iota((slots, feat), 0) < alive[u]
        rows = slice(u * slots, (u + 1) * slots)
        out[u] = jnp.where(live, total[rows], 0.0).astype(BF16)


struct = jax.ShapeDtypeStruct


def in_hbm(a):
    return pltpu.with_memory_space_constraint(a, pltpu.HBM)


def attention(kept, parent, gain, state, wq, wk, wv, wo, keys, values, past_keys, past_values):
    users, slots, width = state.shape
    feat = wq.shape[1]
    history = keys.shape[1]
    steps = past_keys.shape[2]
    rows = users * slots
    return call(
        attention_kernel,
        (struct((rows, feat), F32), struct((rows, feat), F32), struct((rows, 2 * feat), BF16)),
        [IN_HBM] * 12,
        40,
        3_300_000_000,
        20_000_000,
        [
            pltpu.VMEM(kept.shape, jnp.int32),
            pltpu.VMEM(parent.shape, jnp.int32),
            pltpu.VMEM(gain.shape, F32),
            pltpu.VMEM((users, slots, width), BF16),
            pltpu.VMEM((users, slots, feat), BF16),
            pltpu.VMEM((width, feat), BF16),
            pltpu.VMEM((width, feat), BF16),
            pltpu.VMEM((width, feat), BF16),
            pltpu.VMEM((feat, width), BF16),
            pltpu.VMEM((users, history, feat), BF16),
            pltpu.VMEM((users, history, feat), BF16),
            pltpu.VMEM((users, slots * steps, feat), BF16),
            pltpu.VMEM((users, slots * steps, feat), BF16),
            pltpu.VMEM((rows, width), BF16),
            pltpu.VMEM((rows, feat), BF16),
            pltpu.VMEM((rows, feat), BF16),
            pltpu.VMEM((rows, feat), BF16),
            pltpu.VMEM((rows, feat), BF16),
            pltpu.VMEM((rows, feat), BF16),
            pltpu.VMEM((2, 2 * slots, history), F32),
            pltpu.SemaphoreType.DMA((20 + 12 * users,)),
        ],
        2_200_000,
    )(
        *[
            in_hbm(a)
            for a in (
                kept, parent, gain, state, wq, wk, wv, wo, keys, values, past_keys, past_values,
            )
        ]
    )


def route(alive, choice, experts):
    users, top, slots = choice.shape
    rows = users * slots
    return call(
        routing_kernel,
        (struct((6 * 8 * experts, rows), BF16), struct((8, rows), jnp.int32)),
        [IN_SMEM, WHOLE],
        16,
        10_000_000,
        1_000_000,
    )(alive, choice)


def dispatch(keep, from_core, from_z, gain, place):
    rows, feat = keep.shape
    span = place.shape[0] // 3
    return call(
        dispatch_kernel,
        (struct((rows, feat), F32), pltpu.HBM((2 * span, feat * 3 // 2), BF16)),
        [WHOLE] * 5,
        16,
        300_000_000,
        4_000_000,
        [pltpu.VMEM((span, feat * 3 // 2), BF16), pltpu.SemaphoreType.DMA((4,))],
        out_specs=(WHOLE, IN_HBM),
    )(keep, from_core, from_z, gain, place)


def chosen_logits(resid, gain, router, choice):
    return call(
        router_kernel, struct((8, resid.shape[0]), F32), [WHOLE] * 4, 16, 30_000_000, 1_000_000
    )(resid, gain, router, choice)


def gate_matrix(parts, where, experts):
    return call(
        gate_kernel,
        struct((where.shape[1], 6 * 8 * experts), BF16),
        [WHOLE] * 5,
        16,
        3_000_000,
        1_000_000,
    )(*parts, where)


def run_expert(arrived, gain, weights):
    _, width, hidden = weights[0].shape
    rows = arrived.shape[0] // 8 * 3
    return call(
        expert_kernel,
        pltpu.HBM(arrived.shape, BF16),
        [WHOLE] * 2 + [IN_HBM] * 6,
        40,
        4_800_000_000,
        16_000_000,
        [
            pltpu.VMEM((width, hidden), BF16),
            pltpu.VMEM((width, hidden), BF16),
            pltpu.VMEM((width, hidden), BF16),
            pltpu.VMEM((width, hidden), BF16),
            pltpu.VMEM((2 * hidden, width), BF16),
            pltpu.VMEM((rows, width), BF16),
            pltpu.VMEM((rows, 2 * hidden), BF16),
            pltpu.VMEM(arrived.shape, BF16),
            pltpu.SemaphoreType.DMA((24,)),
            pltpu.SemaphoreType.DMA((16,)),
        ],
        400_000,
        IN_HBM,
    )(arrived, gain, *[in_hbm(w) for w in weights])


def combine(alive, resid, gates, returned, users):
    rows, feat = resid.shape
    return call(
        combine_kernel,
        struct((users, rows // users, feat), BF16),
        [IN_SMEM] + [WHOLE] * 3,
        24,
        600_000_000,
        4_000_000,
    )(alive, resid, gates, returned)


def on_device(
    candidate_hidden_states,
    kept_candidate_index,
    slot_parent_beam,
    alive_slot_counts,
    slot_expert_index,
    attention_norm_gain,
    query_projection_weight,
    key_projection_weight,
    value_projection_weight,
    attention_output_weight,
    history_event_keys,
    history_event_values,
    decoded_beam_keys,
    decoded_beam_values,
    expert_norm_gain,
    router_projection_weight,
    expert_gate_weight,
    expert_up_weight,
    expert_down_weight,
):
    users, slots, width = candidate_hidden_states.shape
    feat = query_projection_weight.shape[1]
    experts = router_projection_weight.shape[1]
    core = [(s, s ^ 1) for s in range(4)]
    z_far = [(s, s ^ 2) for s in range(4)]
    both = [(s, s ^ 3) for s in range(4)]
    everyone = ("sec", "dp")

    attention_gain = attention_norm_gain.reshape(1, width)
    expert_gain = expert_norm_gain.reshape(1, width)
    choice = jnp.swapaxes(slot_expert_index, 1, 2)
    router = router_projection_weight.T

    with jax.named_scope("attention"):
        keep_own, keep_other, send = attention(
            kept_candidate_index, slot_parent_beam, attention_gain, candidate_hidden_states,
            query_projection_weight, key_projection_weight, value_projection_weight,
            attention_output_weight, history_event_keys, history_event_values,
            decoded_beam_keys, decoded_beam_values,
        )
    with jax.named_scope("head_sum"):
        from_core = lax.ppermute(send, "sec", core)
        to_z = (keep_other + from_core[:, feat:].astype(F32)).astype(BF16)
        from_z = lax.ppermute(to_z, "sec", z_far)
    with jax.named_scope("routing"):
        place, where = route(alive_slot_counts, choice, experts)
    with jax.named_scope("sibling_weights"):
        weights = [expert_gate_weight, expert_up_weight, expert_down_weight]
        late = lax.optimization_barrier((*weights, where))[:3]
        weights = weights + [lax.ppermute(w, "sec", core) for w in late]
    with jax.named_scope("dispatch"):
        resid, message = dispatch(keep_own, from_core, from_z, expert_gain, place)
        arrived = lax.all_to_all(message, everyone, 0, 0, tiled=True)
    with jax.named_scope("router"):
        part = chosen_logits(resid, expert_gain, router, choice)
        parts = [part] + [lax.ppermute(part, "sec", pairs) for pairs in (core, z_far, both)]
    with jax.named_scope("gates"):
        gates = gate_matrix(parts, where, experts)
    with jax.named_scope("experts"):
        result = run_expert(arrived, expert_gain, weights)
        returned = lax.all_to_all(result, everyone, 0, 0, tiled=True)
    with jax.named_scope("combine"):
        return combine(alive_slot_counts, resid, gates, returned, users)


def solution(mesh):
    in_specs = (
        P("dp", None, None),
        P("dp", None),
        P("dp", None),
        P("dp"),
        P("dp", None, None),
        P(),
        P(None, "sec"),
        P(None, "sec"),
        P(None, "sec"),
        P("sec", None),
        P("dp", None, "sec"),
        P("dp", None, "sec"),
        P("dp", None, None, "sec"),
        P("dp", None, None, "sec"),
        P(),
        P(),
        P("dp", None, "sec"),
        P("dp", None, "sec"),
        P("dp", "sec", None),
    )
    out_specs = P("dp", None, "sec")
    return jax.shard_map(
        on_device, mesh=mesh, in_specs=in_specs, out_specs=out_specs, check_vma=False
    )
```

```python
import functools
import math

import jax
import jax.numpy as jnp
from jax import lax
from jax.experimental import pallas as pl
from jax.experimental.pallas import tpu as pltpu
from jax.sharding import PartitionSpec as P

HD = 128
EPSILON = 1e-05
BF16 = jnp.bfloat16
F32 = jnp.float32
MIB = 1024 * 1024
WHOLE = pl.BlockSpec(memory_space=pltpu.VMEM)
IN_HBM = pl.BlockSpec(memory_space=pl.ANY)


def mm(a, b):
    return jnp.dot(a, b, preferred_element_type=F32)


def mm_nt(a, b):
    return lax.dot_general(a, b, (((1,), (1,)), ((), ())), preferred_element_type=F32)


def iota(shape, dim):
    return lax.broadcasted_iota(jnp.int32, shape, dim)


def call(kernel, out, in_specs, vmem_mib, flops, nbytes, scratch=(), transcendentals=0, out_specs=None):
    return pl.pallas_call(
        kernel,
        out_shape=out,
        in_specs=in_specs,
        out_specs=jax.tree.map(lambda _: WHOLE, out) if out_specs is None else out_specs,
        scratch_shapes=list(scratch),
        compiler_params=pltpu.CompilerParams(vmem_limit_bytes=vmem_mib * MIB),
        cost_estimate=pl.CostEstimate(
            flops=flops, bytes_accessed=nbytes, transcendentals=transcendentals
        ),
    )


class Loads:
    def __init__(self, sems):
        self.sems = sems
        self.copies, self.count = {}, 0

    def start(self, name, *pieces):
        for src, dst in pieces:
            copy = pltpu.make_async_copy(src, dst, self.sems.at[self.count])
            copy.start()
            self.copies.setdefault(name, []).append(copy)
            self.count += 1

    def start_rows(self, name, src, dst, pieces):
        size = dst.shape[0] // pieces
        cuts = [pl.ds(n * size, size) for n in range(pieces)]
        self.start(name, *[(src.at[cut], dst.at[cut]) for cut in cuts])

    def wait(self, name):
        for copy in self.copies[name]:
            copy.wait()


def attention_kernel(
    kept_h, parent_h, gain_h, state_h, wq_h, wk_h, wv_h, wo_h, kh_h, vh_h, dk_h, dv_h,
    keep_own, keep_other, send,
    kept, parent, gain, st, sq, wq, wk, wv, wo, kh, vh, dk, dv, nrm, q, k, v, own, att, scores, sems,
):
    users, slots, width = st.shape
    history = kh.shape[1]
    feat = wq.shape[1]
    heads = feat // HD
    sec = lax.axis_index("sec")
    z, c = sec // 2, sec % 2

    def quarter(n):
        return pl.ds(pl.multiple_of(n * feat, feat), feat)

    order = (sec, 2 * (1 - z) + c, 2 * z + 1 - c, 2 * (1 - z) + 1 - c)
    loads = Loads(sems)
    loads.start("small", (kept_h, kept), (parent_h, parent), (gain_h, gain))
    for u in range(users):
        loads.start_rows(("st", u), state_h.at[u], st.at[u], 2)
    loads.start_rows("wq", wq_h, wq, 4)
    loads.start_rows("wk", wk_h, wk, 4)
    loads.start_rows("wv", wv_h, wv, 4)
    for u in range(users):
        loads.start(
            ("past", u),
            (dk_h.at[u].reshape(dk.shape[1:]), dk.at[u]),
            (dv_h.at[u].reshape(dv.shape[1:]), dv.at[u]),
        )
        loads.start_rows(("kh", u), kh_h.at[u], kh.at[u], 4)
        loads.start_rows(("vh", u), vh_h.at[u], vh.at[u], 4)
    loads.start("sq", (state_h.at[:, :, quarter(sec)], sq))
    loads.start("wo", *[
        (wo_h.at[:, quarter(n)], wo.at[:, pl.ds(at * feat, feat)]) for at, n in enumerate(order)
    ])

    loads.wait("small")
    picks = []
    for u in range(users):
        rows = pl.ds(u * slots, slots)
        picks.append((iota((slots, slots), 0) == kept[u : u + 1, :]).astype(F32).T.astype(BF16))
        loads.wait(("st", u))
        xu = mm(picks[u], st[u])
        mean = jnp.mean(xu * xu, axis=-1, keepdims=True)
        nrm[rows, :] = (xu * lax.rsqrt(mean + EPSILON) * gain[...]).astype(BF16)
    loads.wait("wq")
    q[...] = mm(nrm[...], wq[...]).astype(BF16)
    loads.wait("wk")
    k[...] = mm(nrm[...], wk[...]).astype(BF16)
    loads.wait("wv")
    v[...] = mm(nrm[...], wv[...]).astype(BF16)

    scale = HD ** (-0.5) * math.log2(math.e)
    steps = dk.shape[1] // slots
    chunk = 512
    chunks = [slice(a, a + chunk) for a in range(0, history, chunk)]
    group = 2
    tall, wide = group * slots, group * HD
    sets = [(u, h) for u in range(users) for h in range(0, heads, group)]
    past = {}
    ready = {}

    def stack(f):
        return jnp.concatenate([f(slice(m * HD, (m + 1) * HD)) for m in range(group)], axis=0)

    for n in range(len(sets) + 1):
        if n < len(sets):
            u, h = sets[n]
            rows = pl.ds(u * slots, slots)
            cols = slice(h * HD, h * HD + wide)
            if h == 0:
                loads.wait(("past", u))
                past[u] = []
                for s in range(steps):
                    hot = iota((steps * slots, slots), 0) == parent[u : u + 1, :] * steps + s
                    pick = hot.astype(F32).T.astype(BF16)
                    past[u].append((mm(pick, dk[u]), mm(pick, dv[u])))
                loads.wait(("kh", u))
                loads.wait(("vh", u))
            qs = q[rows, cols]
            blank = jnp.zeros((slots, HD), BF16)
            diagonal = jnp.concatenate(
                [
                    jnp.concatenate(
                        [qs[:, m * HD : (m + 1) * HD] if m == at else blank for m in range(group)], axis=1
                    )
                    for at in range(group)
                ],
                axis=0,
            )
            qf = qs.astype(F32)
            more = []
            for p in [p for p, _ in past[u]] + [k[rows, :].astype(F32)]:
                both = qf * p[:, cols]
                more.append(stack(lambda m: jnp.sum(both[:, m], axis=-1, keepdims=True)))
            high = jnp.full((tall, HD), -jnp.inf, F32)
        if n > 0:
            u0, h0, more0, top = ready.pop(n - 1)
            rows0 = pl.ds(u0 * slots, slots)
            cols0 = slice(h0 * HD, h0 * HD + wide)
            mass = jnp.zeros((tall, HD), F32)
            mixed = jnp.zeros((tall, wide), F32)
        for at in chunks:
            if n < len(sets):
                s = mm_nt(diagonal, kh[u, at, cols])
                scores[n % 2, :, at] = s
                for a in range(0, chunk, HD):
                    high = jnp.maximum(high, s[:, a : a + HD])
            if n > 0:
                e = jnp.exp2((scores[(n - 1) % 2, :, at] - top) * scale)
                for a in range(0, chunk, HD):
                    mass = mass + e[:, a : a + HD]
                mixed = mixed + mm(e.astype(BF16), vh[u0, at, cols0])
        if n < len(sets):
            peak = jnp.max(high, axis=-1, keepdims=True)
            for s in more:
                peak = jnp.maximum(peak, s)
            ready[n] = (u, h, more, peak)
        if n > 0:
            total = jnp.sum(mass, axis=-1, keepdims=True)
            mixed = jnp.concatenate(
                [mixed[m * slots : (m + 1) * slots, m * HD : (m + 1) * HD] for m in range(group)], axis=0
            )
            values = [p[:, cols0] for _, p in past[u0]] + [v[rows0, cols0].astype(F32)]
            for s, value in zip(more0, values):
                e = jnp.exp2((s - top) * scale)
                total = total + e
                mixed = mixed + e * stack(lambda m: value[:, m])
            mixed = (mixed / total).astype(BF16)
            att[rows0, cols0] = jnp.concatenate(
                [mixed[m * slots : (m + 1) * slots] for m in range(group)], axis=1
            )

    loads.wait("sq")
    for u in range(users):
        own[pl.ds(u * slots, slots), :] = mm(picks[u], sq[u]).astype(BF16)
    loads.wait("wo")
    out = mm(att[...], wo[...])
    keep_own[...] = out[:, :feat] + own[...].astype(F32)
    keep_other[...] = out[:, feat : 2 * feat]
    send[...] = out[:, 2 * feat :].astype(BF16)


def routing_kernel(alive, choice, place, where):
    users, top, slots = choice.shape
    rows = users * slots
    lane = iota((1, slots), 1)
    live = jnp.concatenate([lane < alive[:, u : u + 1] for u in range(users)], axis=1)
    experts = place.shape[0] // (6 * 8)
    earlier = (iota((rows, rows), 0) < iota((rows, rows), 1)).astype(F32).astype(BF16)
    base = jnp.zeros((experts, 1), F32)
    main, extra = [], []
    for t in range(top):
        e = jnp.concatenate([choice[u, t : t + 1, :] for u in range(users)], axis=1)
        hot = ((iota((experts, rows), 0) == e) & live).astype(F32)
        before = mm(hot.astype(BF16), earlier)
        rank = jnp.sum(hot * (before + base), axis=0, keepdims=True).astype(jnp.int32)
        base = base + jnp.sum(hot, axis=1, keepdims=True)
        over = rank - 16
        main.append(
            jnp.where(live & (rank < 16), (rank >> 3) * (experts * 8) + e * 8 + (rank & 7), -1)
        )
        extra.append(
            jnp.where(live & (rank >= 16), (over >> 2) * (experts * 8) + e * 8 + (over & 3), -8)
        )
    span = 2 * experts * 8
    index = iota((span, rows), 0)
    for part, (a, b) in enumerate(
        ((main[0], main[1]), (extra[0], extra[1]), (extra[0] + 4, extra[1] + 4))
    ):
        hit = (index == a) | (index == b)
        place[part * span : (part + 1) * span, :] = hit.astype(F32).astype(BF16)
    blank = jnp.zeros((4, rows), jnp.int32)
    where[...] = jnp.concatenate(main + extra + [blank], axis=0)


def dispatch_kernel(keep, from_core, from_z, gain, place, resid, message, block, sems):
    feat = keep.shape[1]
    half = feat // 2
    span = place.shape[0] // 3
    part = span // 2
    sec = lax.axis_index("sec")
    r = keep[...] + from_core[:, :feat].astype(F32) + from_z[...].astype(F32)
    scaled = (r * gain[:, pl.ds(pl.multiple_of(sec * feat, feat), feat)]).astype(BF16)
    copies = []
    for n in range(2):
        rows = slice(n * part, (n + 1) * part)
        block[rows, :feat] = mm(place[rows, :], scaled).astype(BF16)
        folded = mm(place[span + n * part : span + (n + 1) * part, :], scaled[:, :half])
        folded = folded + mm(
            place[2 * span + n * part : 2 * span + (n + 1) * part, :], scaled[:, half:]
        )
        block[rows, feat:] = folded.astype(BF16)
        for z in range(2):
            copies.append(
                pltpu.make_async_copy(
                    block.at[pl.ds(n * part, part)],
                    message.at[pl.ds(z * span + n * part, part)],
                    sems.at[len(copies)],
                )
            )
            copies[-1].start()
    resid[...] = r
    for copy in copies:
        copy.wait()


def router_kernel(resid, gain, router, choice, part):
    users, top, slots = choice.shape
    rows = users * slots
    feat = resid.shape[1]
    experts = router.shape[0]
    sec = lax.axis_index("sec")
    cols = pl.ds(pl.multiple_of(sec * feat, feat), feat)
    r = resid[...]
    scaled = (r * gain[:, cols]).astype(BF16)
    logits = mm_nt(router[:, cols], scaled)
    out = []
    for t in range(top):
        e = jnp.concatenate([choice[u, t : t + 1, :] for u in range(users)], axis=1)
        hot = (iota((experts, rows), 0) == e).astype(F32)
        out.append(jnp.sum(hot * logits, axis=0, keepdims=True))
    squares = lax.dot_general(
        jnp.ones((8, feat), F32), r * r, (((1,), (1,)), ((), ())),
        precision=lax.Precision.HIGHEST, preferred_element_type=F32,
    )
    part[...] = jnp.concatenate(out + [squares[: 8 - top]], axis=0)


def gate_kernel(p0, p1, p2, p3, where, gates):
    rows = where.shape[1]
    total = (p0[...] + p1[...]) + (p2[...] + p3[...])
    width = gates.shape[1] // 3 * 4
    scale = lax.rsqrt(total[2:3] / width + EPSILON)
    sig = [1.0 / (1.0 + jnp.exp(-(total[t : t + 1] * scale))) for t in range(2)]
    weight = [s / (sig[0] + sig[1]) for s in sig]
    span = gates.shape[1] // 3
    index = iota((span, rows), 0)
    for part, shift in enumerate((0, 0, 4)):
        first = 0 if part == 0 else 2
        g = jnp.where(index == where[first : first + 1, :] + shift, weight[0], 0.0)
        g = jnp.where(index == where[first + 1 : first + 2, :] + shift, weight[1], g)
        gates[:, part * span : (part + 1) * span] = g.T.astype(BF16)


def unfold(folded):
    rows, width = folded.shape
    pair = folded.astype(F32).reshape(rows // 16, 2, 8, width)
    a, b = pair[:, 0], pair[:, 1]
    first = iota(a.shape, 1) < 4
    left = jnp.where(first, a, pltpu.roll(b, 4, 1))
    right = jnp.where(first, pltpu.roll(a, 4, 1), b)
    return [t.reshape(rows // 2, width).astype(BF16) for t in (left, right)]


def fold(left, right):
    rows, width = left.shape
    left, right = (t.reshape(rows // 8, 8, width) for t in (left, right))
    first = iota(left.shape, 1) < 4
    a = jnp.where(first, left, pltpu.roll(right, 4, 1))
    b = jnp.where(first, pltpu.roll(left, 4, 1), right)
    return jnp.stack([a, b], axis=1).reshape(rows * 2, width)


def expert_kernel(
    arrived, gain, wg0_h, wu0_h, wd0_h, wg1_h, wu1_h, wd1_h, message,
    wg0, wu0, wg1, wu1, wd, x, act, block, sems, out_sems,
):
    width, hidden = wg0.shape
    quarters = 4
    feat = width // quarters
    half = feat // 2
    part = arrived.shape[0] // quarters
    loads = Loads(sems)
    for n, (src, dst) in enumerate(((wg0_h, wg0), (wu0_h, wu0), (wg1_h, wg1), (wu1_h, wu1))):
        loads.start_rows(n, src.at[0], dst, 4)
    loads.start_rows(4, wd0_h.at[0], wd.at[pl.ds(0, hidden)], 4)
    loads.start_rows(5, wd1_h.at[0], wd.at[pl.ds(hidden, hidden)], 4)
    for p in range(quarters):
        rows = slice(p * part, (p + 1) * part)
        x[:part, p * feat : (p + 1) * feat] = arrived[rows, :feat]
        for n, piece in enumerate(unfold(arrived[rows, feat:])):
            at = p * feat + n * half
            x[part:, at : at + half] = piece
    plain = x[...].astype(F32) * (1.0 / gain[...])
    scale = lax.rsqrt(jnp.mean(plain * plain, axis=-1, keepdims=True) + EPSILON)
    for n, (wg, wu) in enumerate(((wg0, wu0), (wg1, wu1))):
        loads.wait(2 * n)
        g = mm(x[...], wg[...]) * scale
        loads.wait(2 * n + 1)
        u = mm(x[...], wu[...]) * scale
        act[:, n * hidden : (n + 1) * hidden] = (g / (1.0 + jnp.exp(-g)) * u).astype(BF16)
    loads.wait(4)
    loads.wait(5)
    copies = []
    for p in range(quarters):
        cols = slice(p * feat, (p + 1) * feat)
        rows = slice(p * part, (p + 1) * part)
        y = mm(act[...], wd[:, cols])
        block[rows, :feat] = y[:part].astype(BF16)
        block[rows, feat:] = fold(y[part:, :half], y[part:, half:]).astype(BF16)
        for n in range(4):
            here = pl.ds(p * part + n * (part // 4), part // 4)
            copies.append(
                pltpu.make_async_copy(block.at[here], message.at[here], out_sems.at[len(copies)])
            )
            copies[-1].start()
    for copy in copies:
        copy.wait()


def combine_kernel(alive, resid, gates, arrived, out):
    users, slots, feat = out.shape
    span = gates.shape[1] // 3

    def bring(part, cols):
        g = gates[:, part * span : (part + 1) * span]
        return mm(jnp.concatenate([g, g], axis=1), arrived[:, cols])

    main = bring(0, slice(0, feat))
    tail = slice(feat, arrived.shape[1])
    total = resid[...] + main + jnp.concatenate([bring(1, tail), bring(2, tail)], axis=1)
    for u in range(users):
        live = iota((slots, feat), 0) < alive[:, u : u + 1]
        rows = slice(u * slots, (u + 1) * slots)
        out[u] = jnp.where(live, total[rows], 0.0).astype(BF16)


struct = jax.ShapeDtypeStruct


def in_hbm(a):
    return pltpu.with_memory_space_constraint(a, pltpu.HBM)


def attention(kept, parent, gain, state, wq, wk, wv, wo, keys, values, past_keys, past_values):
    users, slots, width = state.shape
    feat = wq.shape[1]
    history = keys.shape[1]
    steps = past_keys.shape[2]
    rows = users * slots
    return call(
        attention_kernel,
        (struct((rows, feat), F32), struct((rows, feat), F32), struct((rows, 2 * feat), BF16)),
        [IN_HBM] * 12,
        40,
        3_300_000_000,
        20_000_000,
        [
            pltpu.VMEM(kept.shape, jnp.int32),
            pltpu.VMEM(parent.shape, jnp.int32),
            pltpu.VMEM(gain.shape, F32),
            pltpu.VMEM((users, slots, width), BF16),
            pltpu.VMEM((users, slots, feat), BF16),
            pltpu.VMEM((width, feat), BF16),
            pltpu.VMEM((width, feat), BF16),
            pltpu.VMEM((width, feat), BF16),
            pltpu.VMEM((feat, width), BF16),
            pltpu.VMEM((users, history, feat), BF16),
            pltpu.VMEM((users, history, feat), BF16),
            pltpu.VMEM((users, slots * steps, feat), BF16),
            pltpu.VMEM((users, slots * steps, feat), BF16),
            pltpu.VMEM((rows, width), BF16),
            pltpu.VMEM((rows, feat), BF16),
            pltpu.VMEM((rows, feat), BF16),
            pltpu.VMEM((rows, feat), BF16),
            pltpu.VMEM((rows, feat), BF16),
            pltpu.VMEM((rows, feat), BF16),
            pltpu.VMEM((2, 2 * slots, history), F32),
            pltpu.SemaphoreType.DMA((20 + 12 * users,)),
        ],
        2_200_000,
    )(
        *[
            in_hbm(a)
            for a in (
                kept, parent, gain, state, wq, wk, wv, wo, keys, values, past_keys, past_values,
            )
        ]
    )


def route(alive, choice, experts):
    users, top, slots = choice.shape
    rows = users * slots
    return call(
        routing_kernel,
        (struct((6 * 8 * experts, rows), BF16), struct((8, rows), jnp.int32)),
        [WHOLE] * 2,
        16,
        10_000_000,
        1_000_000,
    )(alive, choice)


def dispatch(keep, from_core, from_z, gain, place):
    rows, feat = keep.shape
    span = place.shape[0] // 3
    return call(
        dispatch_kernel,
        (struct((rows, feat), F32), pltpu.HBM((2 * span, feat * 3 // 2), BF16)),
        [WHOLE] * 5,
        16,
        300_000_000,
        4_000_000,
        [pltpu.VMEM((span, feat * 3 // 2), BF16), pltpu.SemaphoreType.DMA((4,))],
        out_specs=(WHOLE, IN_HBM),
    )(keep, from_core, from_z, gain, place)


def chosen_logits(resid, gain, router, choice):
    return call(
        router_kernel, struct((8, resid.shape[0]), F32), [WHOLE] * 4, 16, 30_000_000, 1_000_000
    )(resid, gain, router, choice)


def gate_matrix(parts, where, experts):
    return call(
        gate_kernel,
        struct((where.shape[1], 6 * 8 * experts), BF16),
        [WHOLE] * 5,
        16,
        3_000_000,
        1_000_000,
    )(*parts, where)


def run_expert(arrived, gain, weights):
    _, width, hidden = weights[0].shape
    rows = arrived.shape[0] // 8 * 3
    return call(
        expert_kernel,
        pltpu.HBM(arrived.shape, BF16),
        [WHOLE] * 2 + [IN_HBM] * 6,
        40,
        4_800_000_000,
        16_000_000,
        [
            pltpu.VMEM((width, hidden), BF16),
            pltpu.VMEM((width, hidden), BF16),
            pltpu.VMEM((width, hidden), BF16),
            pltpu.VMEM((width, hidden), BF16),
            pltpu.VMEM((2 * hidden, width), BF16),
            pltpu.VMEM((rows, width), BF16),
            pltpu.VMEM((rows, 2 * hidden), BF16),
            pltpu.VMEM(arrived.shape, BF16),
            pltpu.SemaphoreType.DMA((24,)),
            pltpu.SemaphoreType.DMA((16,)),
        ],
        400_000,
        IN_HBM,
    )(arrived, gain, *[in_hbm(w) for w in weights])


def combine(alive, resid, gates, returned, users):
    rows, feat = resid.shape
    return call(
        combine_kernel,
        struct((users, rows // users, feat), BF16),
        [WHOLE] * 4,
        24,
        600_000_000,
        4_000_000,
    )(alive, resid, gates, returned)


def on_device(
    candidate_hidden_states,
    kept_candidate_index,
    slot_parent_beam,
    alive_slot_counts,
    slot_expert_index,
    attention_norm_gain,
    query_projection_weight,
    key_projection_weight,
    value_projection_weight,
    attention_output_weight,
    history_event_keys,
    history_event_values,
    decoded_beam_keys,
    decoded_beam_values,
    expert_norm_gain,
    router_projection_weight,
    expert_gate_weight,
    expert_up_weight,
    expert_down_weight,
):
    users, slots, width = candidate_hidden_states.shape
    feat = query_projection_weight.shape[1]
    experts = router_projection_weight.shape[1]
    core = [(s, s ^ 1) for s in range(4)]
    z_far = [(s, s ^ 2) for s in range(4)]
    both = [(s, s ^ 3) for s in range(4)]
    everyone = ("sec", "dp")

    attention_gain = attention_norm_gain.reshape(1, width)
    expert_gain = expert_norm_gain.reshape(1, width)
    alive = alive_slot_counts.reshape(1, users)
    choice = jnp.swapaxes(slot_expert_index, 1, 2)
    router = router_projection_weight.T

    with jax.named_scope("attention"):
        keep_own, keep_other, send = attention(
            kept_candidate_index, slot_parent_beam, attention_gain, candidate_hidden_states,
            query_projection_weight, key_projection_weight, value_projection_weight,
            attention_output_weight, history_event_keys, history_event_values,
            decoded_beam_keys, decoded_beam_values,
        )
    with jax.named_scope("head_sum"):
        from_core = lax.ppermute(send, "sec", core)
        to_z = (keep_other + from_core[:, feat:].astype(F32)).astype(BF16)
        from_z = lax.ppermute(to_z, "sec", z_far)
    with jax.named_scope("routing"):
        place, where = route(alive, choice, experts)
    with jax.named_scope("sibling_weights"):
        weights = [expert_gate_weight, expert_up_weight, expert_down_weight]
        late = lax.optimization_barrier((*weights, to_z))[:3]
        weights = weights + [lax.ppermute(w, "sec", core) for w in late]
    with jax.named_scope("dispatch"):
        resid, message = dispatch(keep_own, from_core, from_z, expert_gain, place)
        arrived = lax.all_to_all(message, everyone, 0, 0, tiled=True)
    with jax.named_scope("router"):
        part = chosen_logits(resid, expert_gain, router, choice)
        parts = [part] + [lax.ppermute(part, "sec", pairs) for pairs in (core, z_far, both)]
    with jax.named_scope("gates"):
        gates = gate_matrix(parts, where, experts)
    with jax.named_scope("experts"):
        result = run_expert(arrived, expert_gain, weights)
        returned = lax.all_to_all(result, everyone, 0, 0, tiled=True)
    with jax.named_scope("combine"):
        return combine(alive, resid, gates, returned, users)


def solution(mesh):
    in_specs = (
        P("dp", None, None),
        P("dp", None),
        P("dp", None),
        P("dp"),
        P("dp", None, None),
        P(),
        P(None, "sec"),
        P(None, "sec"),
        P(None, "sec"),
        P("sec", None),
        P("dp", None, "sec"),
        P("dp", None, "sec"),
        P("dp", None, None, "sec"),
        P("dp", None, None, "sec"),
        P(),
        P(),
        P("dp", None, "sec"),
        P("dp", None, "sec"),
        P("dp", "sec", None),
    )
    out_specs = P("dp", None, "sec")
    return jax.shard_map(
        on_device, mesh=mesh, in_specs=in_specs, out_specs=out_specs, check_vma=False
    )
```

```python
import functools
import math

import jax
import jax.numpy as jnp
from jax import lax
from jax.experimental import pallas as pl
from jax.experimental.pallas import tpu as pltpu
from jax.sharding import PartitionSpec as P

HD = 128
EPSILON = 1e-05
BF16 = jnp.bfloat16
F32 = jnp.float32
MIB = 1024 * 1024
WHOLE = pl.BlockSpec(memory_space=pltpu.VMEM)
IN_HBM = pl.BlockSpec(memory_space=pl.ANY)


def mm(a, b):
    return jnp.dot(a, b, preferred_element_type=F32)


def mm_nt(a, b):
    return lax.dot_general(a, b, (((1,), (1,)), ((), ())), preferred_element_type=F32)


def iota(shape, dim):
    return lax.broadcasted_iota(jnp.int32, shape, dim)


def call(kernel, out, in_specs, vmem_mib, flops, nbytes, scratch=(), transcendentals=0, out_specs=None):
    return pl.pallas_call(
        kernel,
        out_shape=out,
        in_specs=in_specs,
        out_specs=jax.tree.map(lambda _: WHOLE, out) if out_specs is None else out_specs,
        scratch_shapes=list(scratch),
        compiler_params=pltpu.CompilerParams(vmem_limit_bytes=vmem_mib * MIB),
        cost_estimate=pl.CostEstimate(
            flops=flops, bytes_accessed=nbytes, transcendentals=transcendentals
        ),
    )


class Loads:
    def __init__(self, sems):
        self.sems = sems
        self.copies, self.count = {}, 0

    def start(self, name, *pieces):
        for src, dst in pieces:
            copy = pltpu.make_async_copy(src, dst, self.sems.at[self.count])
            copy.start()
            self.copies.setdefault(name, []).append(copy)
            self.count += 1

    def start_rows(self, name, src, dst, pieces):
        size = dst.shape[0] // pieces
        cuts = [pl.ds(n * size, size) for n in range(pieces)]
        self.start(name, *[(src.at[cut], dst.at[cut]) for cut in cuts])

    def wait(self, name):
        for copy in self.copies[name]:
            copy.wait()


def attention_kernel(
    kept_h, parent_h, gain_h, state_h, wq_h, wk_h, wv_h, wo_h, kh_h, vh_h, dk_h, dv_h,
    keep_own, keep_other, send,
    kept, parent, gain, st, sq, wq, wk, wv, wo, kh, vh, dk, dv, nrm, q, k, v, own, att, scores, sems,
):
    users, slots, width = st.shape
    history = kh.shape[1]
    feat = wq.shape[1]
    heads = feat // HD
    sec = lax.axis_index("sec")
    z, c = sec // 2, sec % 2

    def quarter(n):
        return pl.ds(pl.multiple_of(n * feat, feat), feat)

    loads = Loads(sems)
    loads.start("small", (kept_h, kept), (parent_h, parent), (gain_h, gain))
    for u in range(users):
        loads.start_rows(("st", u), state_h.at[u], st.at[u], 2)
    loads.start_rows("wq", wq_h, wq, 2)
    loads.start_rows("wk", wk_h, wk, 2)
    loads.start_rows("wv", wv_h, wv, 2)
    for u in range(users):
        loads.start(
            ("past", u),
            (dk_h.at[u], dk.at[u]),
            (dv_h.at[u], dv.at[u]),
        )
        loads.start_rows(("kh", u), kh_h.at[u], kh.at[u], 2)
        loads.start_rows(("vh", u), vh_h.at[u], vh.at[u], 2)
    loads.start_rows("wo", wo_h, wo, 2)

    loads.wait("small")
    picks = []
    for u in range(users):
        rows = pl.ds(u * slots, slots)
        picks.append((iota((slots, slots), 0) == kept[u : u + 1, :]).astype(F32).T.astype(BF16))
        loads.wait(("st", u))
        xu = mm(picks[u], st[u])
        mean = jnp.mean(xu * xu, axis=-1, keepdims=True)
        nrm[rows, :] = (xu * lax.rsqrt(mean + EPSILON) * gain[...]).astype(BF16)
    loads.wait("wq")
    q[...] = (mm(nrm[...], wq[...]) * (HD ** (-0.5) * math.log2(math.e))).astype(BF16)
    loads.wait("wk")
    k[...] = mm(nrm[...], wk[...]).astype(BF16)
    loads.wait("wv")
    v[...] = mm(nrm[...], wv[...]).astype(BF16)

    steps = dk.shape[2]
    chunk = 512
    chunks = [slice(a, a + chunk) for a in range(0, history, chunk)]
    group = 2
    tall, wide = group * slots, group * HD
    sets = [(u, h) for u in range(users) for h in range(0, heads, group)]
    past = {}
    ready = {}

    def stack(f):
        return jnp.concatenate([f(slice(m * HD, (m + 1) * HD)) for m in range(group)], axis=0)

    for n in range(len(sets) + 1):
        if n < len(sets):
            u, h = sets[n]
            rows = pl.ds(u * slots, slots)
            cols = slice(h * HD, h * HD + wide)
            if h == 0:
                loads.wait(("past", u))
                past[u] = []
                flat = [t[u].reshape(slots * steps, feat) for t in (dk, dv)]
                for s in range(steps):
                    hot = iota((steps * slots, slots), 0) == parent[u : u + 1, :] * steps + s
                    pick = hot.astype(F32).T.astype(BF16)
                    past[u].append(tuple(mm(pick, t) for t in flat))
                loads.wait(("kh", u))
                loads.wait(("vh", u))
            qs = q[rows, cols]
            blank = jnp.zeros((slots, HD), BF16)
            diagonal = jnp.concatenate(
                [
                    jnp.concatenate(
                        [qs[:, m * HD : (m + 1) * HD] if m == at else blank for m in range(group)], axis=1
                    )
                    for at in range(group)
                ],
                axis=0,
            )
            qf = qs.astype(F32)
            more = []
            for p in [p for p, _ in past[u]] + [k[rows, :].astype(F32)]:
                both = qf * p[:, cols]
                more.append(stack(lambda m: jnp.sum(both[:, m], axis=-1, keepdims=True)))
            high = jnp.full((tall, HD), -jnp.inf, F32)
        if n > 0:
            u0, h0, more0, top = ready.pop(n - 1)
            rows0 = pl.ds(u0 * slots, slots)
            cols0 = slice(h0 * HD, h0 * HD + wide)
            mass = jnp.zeros((tall, HD), F32)
            mixed = jnp.zeros((tall, wide), F32)
        for at in chunks:
            if n < len(sets):
                s = mm_nt(diagonal, kh[u, at, cols])
                scores[n % 2, :, at] = s
                for a in range(0, chunk, HD):
                    high = jnp.maximum(high, s[:, a : a + HD])
            if n > 0:
                e = jnp.exp2(scores[(n - 1) % 2, :, at] - top)
                for a in range(0, chunk, HD):
                    mass = mass + e[:, a : a + HD]
                mixed = mixed + mm(e.astype(BF16), vh[u0, at, cols0])
        if n < len(sets):
            peak = jnp.max(high, axis=-1, keepdims=True)
            for s in more:
                peak = jnp.maximum(peak, s)
            ready[n] = (u, h, more, peak)
        if n > 0:
            total = jnp.sum(mass, axis=-1, keepdims=True)
            mixed = jnp.concatenate(
                [mixed[m * slots : (m + 1) * slots, m * HD : (m + 1) * HD] for m in range(group)], axis=0
            )
            values = [p[:, cols0] for _, p in past[u0]] + [v[rows0, cols0].astype(F32)]
            for s, value in zip(more0, values):
                e = jnp.exp2(s - top)
                total = total + e
                mixed = mixed + e * stack(lambda m: value[:, m])
            mixed = (mixed / total).astype(BF16)
            att[rows0, cols0] = jnp.concatenate(
                [mixed[m * slots : (m + 1) * slots] for m in range(group)], axis=1
            )

    for u in range(users):
        own[pl.ds(u * slots, slots), :] = mm(picks[u], st[u, :, quarter(sec)]).astype(BF16)
    loads.wait("wo")
    keep_own[...] = mm(att[...], wo[:, quarter(sec)]) + own[...].astype(F32)
    keep_other[...] = mm(att[...], wo[:, quarter(2 * (1 - z) + c)])
    send[:, :feat] = mm(att[...], wo[:, quarter(2 * z + 1 - c)]).astype(BF16)
    send[:, feat:] = mm(att[...], wo[:, quarter(2 * (1 - z) + 1 - c)]).astype(BF16)


def routing_kernel(alive, choice, place, where):
    users, top, slots = choice.shape
    rows = users * slots
    lane = iota((1, slots), 1)
    live = jnp.concatenate([lane < alive[:, u : u + 1] for u in range(users)], axis=1)
    experts = place.shape[0] // (6 * 8)
    earlier = (iota((rows, rows), 0) < iota((rows, rows), 1)).astype(F32).astype(BF16)
    base = jnp.zeros((experts, 1), F32)
    main, extra = [], []
    for t in range(top):
        e = jnp.concatenate([choice[u, t : t + 1, :] for u in range(users)], axis=1)
        hot = ((iota((experts, rows), 0) == e) & live).astype(F32)
        before = mm(hot.astype(BF16), earlier)
        rank = jnp.sum(hot * (before + base), axis=0, keepdims=True).astype(jnp.int32)
        base = base + jnp.sum(hot, axis=1, keepdims=True)
        over = rank - 16
        main.append(
            jnp.where(live & (rank < 16), (rank >> 3) * (experts * 8) + e * 8 + (rank & 7), -1)
        )
        extra.append(
            jnp.where(live & (rank >= 16), (over >> 2) * (experts * 8) + e * 8 + (over & 3), -8)
        )
    span = 2 * experts * 8
    index = iota((span, rows), 0)
    for part, (a, b) in enumerate(
        ((main[0], main[1]), (extra[0], extra[1]), (extra[0] + 4, extra[1] + 4))
    ):
        hit = (index == a) | (index == b)
        place[part * span : (part + 1) * span, :] = hit.astype(F32).astype(BF16)
    blank = jnp.zeros((4, rows), jnp.int32)
    where[...] = jnp.concatenate(main + extra + [blank], axis=0)


def dispatch_kernel(keep, from_core, from_z, gain, place, resid, message, block, sems):
    feat = keep.shape[1]
    half = feat // 2
    span = place.shape[0] // 3
    part = span // 2
    sec = lax.axis_index("sec")
    r = keep[...] + from_core[:, :feat].astype(F32) + from_z[...].astype(F32)
    scaled = (r * gain[:, pl.ds(pl.multiple_of(sec * feat, feat), feat)]).astype(BF16)
    copies = []
    for n in range(2):
        rows = slice(n * part, (n + 1) * part)
        block[rows, :feat] = mm(place[rows, :], scaled).astype(BF16)
        folded = mm(place[span + n * part : span + (n + 1) * part, :], scaled[:, :half])
        folded = folded + mm(
            place[2 * span + n * part : 2 * span + (n + 1) * part, :], scaled[:, half:]
        )
        block[rows, feat:] = folded.astype(BF16)
        for z in range(2):
            copies.append(
                pltpu.make_async_copy(
                    block.at[pl.ds(n * part, part)],
                    message.at[pl.ds(z * span + n * part, part)],
                    sems.at[len(copies)],
                )
            )
            copies[-1].start()
    resid[...] = r
    for copy in copies:
        copy.wait()


def router_kernel(resid, gain, router, choice, part):
    users, top, slots = choice.shape
    rows = users * slots
    feat = resid.shape[1]
    experts = router.shape[0]
    sec = lax.axis_index("sec")
    cols = pl.ds(pl.multiple_of(sec * feat, feat), feat)
    r = resid[...]
    scaled = (r * gain[:, cols]).astype(BF16)
    logits = mm_nt(router[:, cols], scaled)
    out = []
    for t in range(top):
        e = jnp.concatenate([choice[u, t : t + 1, :] for u in range(users)], axis=1)
        hot = (iota((experts, rows), 0) == e).astype(F32)
        out.append(jnp.sum(hot * logits, axis=0, keepdims=True))
    squares = lax.dot_general(
        jnp.ones((8, feat), F32), r * r, (((1,), (1,)), ((), ())),
        precision=lax.Precision.HIGHEST, preferred_element_type=F32,
    )
    part[...] = jnp.concatenate(out + [squares[: 8 - top]], axis=0)


def gate_kernel(p0, p1, p2, p3, where, gates):
    rows = where.shape[1]
    total = (p0[...] + p1[...]) + (p2[...] + p3[...])
    width = gates.shape[1] // 3 * 4
    scale = lax.rsqrt(total[2:3] / width + EPSILON)
    sig = [1.0 / (1.0 + jnp.exp(-(total[t : t + 1] * scale))) for t in range(2)]
    weight = [s / (sig[0] + sig[1]) for s in sig]
    span = gates.shape[1] // 3
    index = iota((span, rows), 0)
    for part, shift in enumerate((0, 0, 4)):
        first = 0 if part == 0 else 2
        g = jnp.where(index == where[first : first + 1, :] + shift, weight[0], 0.0)
        g = jnp.where(index == where[first + 1 : first + 2, :] + shift, weight[1], g)
        gates[:, part * span : (part + 1) * span] = g.T.astype(BF16)


def unfold(folded):
    rows, width = folded.shape
    pair = folded.astype(F32).reshape(rows // 16, 2, 8, width)
    a, b = pair[:, 0], pair[:, 1]
    first = iota(a.shape, 1) < 4
    left = jnp.where(first, a, pltpu.roll(b, 4, 1))
    right = jnp.where(first, pltpu.roll(a, 4, 1), b)
    return [t.reshape(rows // 2, width).astype(BF16) for t in (left, right)]


def fold(left, right):
    rows, width = left.shape
    left, right = (t.reshape(rows // 8, 8, width) for t in (left, right))
    first = iota(left.shape, 1) < 4
    a = jnp.where(first, left, pltpu.roll(right, 4, 1))
    b = jnp.where(first, pltpu.roll(left, 4, 1), right)
    return jnp.stack([a, b], axis=1).reshape(rows * 2, width)


def expert_kernel(
    arrived, gain, wg0_h, wu0_h, wd0_h, wg1_h, wu1_h, wd1_h, message,
    wg0, wu0, wg1, wu1, wd, x, act, block, sems, out_sems,
):
    width, hidden = wg0.shape
    quarters = 4
    feat = width // quarters
    half = feat // 2
    part = arrived.shape[0] // quarters
    loads = Loads(sems)
    for n, (src, dst) in enumerate(((wg0_h, wg0), (wu0_h, wu0), (wg1_h, wg1), (wu1_h, wu1))):
        loads.start_rows(n, src.at[0], dst, 4)
    loads.start_rows(4, wd0_h.at[0], wd.at[pl.ds(0, hidden)], 4)
    loads.start_rows(5, wd1_h.at[0], wd.at[pl.ds(hidden, hidden)], 4)
    for p in range(quarters):
        rows = slice(p * part, (p + 1) * part)
        x[:part, p * feat : (p + 1) * feat] = arrived[rows, :feat]
        for n, piece in enumerate(unfold(arrived[rows, feat:])):
            at = p * feat + n * half
            x[part:, at : at + half] = piece
    plain = x[...].astype(F32) * (1.0 / gain[...])
    scale = lax.rsqrt(jnp.mean(plain * plain, axis=-1, keepdims=True) + EPSILON)
    for n, (wg, wu) in enumerate(((wg0, wu0), (wg1, wu1))):
        loads.wait(2 * n)
        g = mm(x[...], wg[...]) * scale
        loads.wait(2 * n + 1)
        u = mm(x[...], wu[...]) * scale
        act[:, n * hidden : (n + 1) * hidden] = (g / (1.0 + jnp.exp(-g)) * u).astype(BF16)
    loads.wait(4)
    loads.wait(5)
    copies = []
    for p in range(quarters):
        cols = slice(p * feat, (p + 1) * feat)
        rows = slice(p * part, (p + 1) * part)
        y = mm(act[...], wd[:, cols])
        block[rows, :feat] = y[:part].astype(BF16)
        block[rows, feat:] = fold(y[part:, :half], y[part:, half:]).astype(BF16)
        for n in range(4):
            here = pl.ds(p * part + n * (part // 4), part // 4)
            copies.append(
                pltpu.make_async_copy(block.at[here], message.at[here], out_sems.at[len(copies)])
            )
            copies[-1].start()
    for copy in copies:
        copy.wait()


def combine_kernel(alive, resid, gates, arrived, out):
    users, slots, feat = out.shape
    span = gates.shape[1] // 3

    def bring(part, cols):
        g = gates[:, part * span : (part + 1) * span]
        return mm(jnp.concatenate([g, g], axis=1), arrived[:, cols])

    main = bring(0, slice(0, feat))
    tail = slice(feat, arrived.shape[1])
    total = resid[...] + main + jnp.concatenate([bring(1, tail), bring(2, tail)], axis=1)
    for u in range(users):
        live = iota((slots, feat), 0) < alive[:, u : u + 1]
        rows = slice(u * slots, (u + 1) * slots)
        out[u] = jnp.where(live, total[rows], 0.0).astype(BF16)


struct = jax.ShapeDtypeStruct


def in_hbm(a):
    return pltpu.with_memory_space_constraint(a, pltpu.HBM)


def attention(kept, parent, gain, state, wq, wk, wv, wo, keys, values, past_keys, past_values):
    users, slots, width = state.shape
    feat = wq.shape[1]
    history = keys.shape[1]
    steps = past_keys.shape[2]
    rows = users * slots
    return call(
        attention_kernel,
        (struct((rows, feat), F32), struct((rows, feat), F32), struct((rows, 2 * feat), BF16)),
        [IN_HBM] * 12,
        40,
        3_300_000_000,
        20_000_000,
        [
            pltpu.VMEM(kept.shape, jnp.int32),
            pltpu.VMEM(parent.shape, jnp.int32),
            pltpu.VMEM(gain.shape, F32),
            pltpu.VMEM((users, slots, width), BF16),
            pltpu.VMEM((users, slots, feat), BF16),
            pltpu.VMEM((width, feat), BF16),
            pltpu.VMEM((width, feat), BF16),
            pltpu.VMEM((width, feat), BF16),
            pltpu.VMEM((feat, width), BF16),
            pltpu.VMEM((users, history, feat), BF16),
            pltpu.VMEM((users, history, feat), BF16),
            pltpu.VMEM(past_keys.shape, BF16),
            pltpu.VMEM(past_keys.shape, BF16),
            pltpu.VMEM((rows, width), BF16),
            pltpu.VMEM((rows, feat), BF16),
            pltpu.VMEM((rows, feat), BF16),
            pltpu.VMEM((rows, feat), BF16),
            pltpu.VMEM((rows, feat), BF16),
            pltpu.VMEM((rows, feat), BF16),
            pltpu.VMEM((2, 2 * slots, history), F32),
            pltpu.SemaphoreType.DMA((20 + 12 * users,)),
        ],
        2_200_000,
    )(
        *[
            in_hbm(a)
            for a in (
                kept, parent, gain, state, wq, wk, wv, wo, keys, values, past_keys, past_values,
            )
        ]
    )


def route(alive, choice, experts):
    users, top, slots = choice.shape
    rows = users * slots
    return call(
        routing_kernel,
        (struct((6 * 8 * experts, rows), BF16), struct((8, rows), jnp.int32)),
        [WHOLE] * 2,
        16,
        10_000_000,
        1_000_000,
    )(alive, choice)


def dispatch(keep, from_core, from_z, gain, place):
    rows, feat = keep.shape
    span = place.shape[0] // 3
    return call(
        dispatch_kernel,
        (struct((rows, feat), F32), pltpu.HBM((2 * span, feat * 3 // 2), BF16)),
        [WHOLE] * 5,
        16,
        300_000_000,
        4_000_000,
        [pltpu.VMEM((span, feat * 3 // 2), BF16), pltpu.SemaphoreType.DMA((4,))],
        out_specs=(WHOLE, IN_HBM),
    )(keep, from_core, from_z, gain, place)


def chosen_logits(resid, gain, router, choice):
    return call(
        router_kernel, struct((8, resid.shape[0]), F32), [WHOLE] * 4, 16, 30_000_000, 1_000_000
    )(resid, gain, router, choice)


def gate_matrix(parts, where, experts):
    return call(
        gate_kernel,
        struct((where.shape[1], 6 * 8 * experts), BF16),
        [WHOLE] * 5,
        16,
        3_000_000,
        1_000_000,
    )(*parts, where)


def run_expert(arrived, gain, weights):
    _, width, hidden = weights[0].shape
    rows = arrived.shape[0] // 8 * 3
    return call(
        expert_kernel,
        pltpu.HBM(arrived.shape, BF16),
        [WHOLE] * 2 + [IN_HBM] * 6,
        40,
        4_800_000_000,
        16_000_000,
        [
            pltpu.VMEM((width, hidden), BF16),
            pltpu.VMEM((width, hidden), BF16),
            pltpu.VMEM((width, hidden), BF16),
            pltpu.VMEM((width, hidden), BF16),
            pltpu.VMEM((2 * hidden, width), BF16),
            pltpu.VMEM((rows, width), BF16),
            pltpu.VMEM((rows, 2 * hidden), BF16),
            pltpu.VMEM(arrived.shape, BF16),
            pltpu.SemaphoreType.DMA((24,)),
            pltpu.SemaphoreType.DMA((16,)),
        ],
        400_000,
        IN_HBM,
    )(arrived, gain, *[in_hbm(w) for w in weights])


def combine(alive, resid, gates, returned, users):
    rows, feat = resid.shape
    return call(
        combine_kernel,
        struct((users, rows // users, feat), BF16),
        [WHOLE] * 4,
        24,
        600_000_000,
        4_000_000,
    )(alive, resid, gates, returned)


def on_device(
    candidate_hidden_states,
    kept_candidate_index,
    slot_parent_beam,
    alive_slot_counts,
    slot_expert_index,
    attention_norm_gain,
    query_projection_weight,
    key_projection_weight,
    value_projection_weight,
    attention_output_weight,
    history_event_keys,
    history_event_values,
    decoded_beam_keys,
    decoded_beam_values,
    expert_norm_gain,
    router_projection_weight,
    expert_gate_weight,
    expert_up_weight,
    expert_down_weight,
):
    users, slots, width = candidate_hidden_states.shape
    feat = query_projection_weight.shape[1]
    experts = router_projection_weight.shape[1]
    core = [(s, s ^ 1) for s in range(4)]
    z_far = [(s, s ^ 2) for s in range(4)]
    both = [(s, s ^ 3) for s in range(4)]
    everyone = ("sec", "dp")

    attention_gain = attention_norm_gain.reshape(1, width)
    expert_gain = expert_norm_gain.reshape(1, width)
    alive = alive_slot_counts.reshape(1, users)
    choice = jnp.swapaxes(slot_expert_index, 1, 2)
    router = router_projection_weight.T

    with jax.named_scope("attention"):
        keep_own, keep_other, send = attention(
            kept_candidate_index, slot_parent_beam, attention_gain, candidate_hidden_states,
            query_projection_weight, key_projection_weight, value_projection_weight,
            attention_output_weight, history_event_keys, history_event_values,
            decoded_beam_keys, decoded_beam_values,
        )
    with jax.named_scope("head_sum"):
        from_core = lax.ppermute(send, "sec", core)
        to_z = (keep_other + from_core[:, feat:].astype(F32)).astype(BF16)
        from_z = lax.ppermute(to_z, "sec", z_far)
    with jax.named_scope("routing"):
        place, where = route(alive, choice, experts)
    with jax.named_scope("sibling_weights"):
        weights = [expert_gate_weight, expert_up_weight, expert_down_weight]
        late = lax.optimization_barrier((*weights, where))[:3]
        weights = weights + [lax.ppermute(w, "sec", core) for w in late]
    with jax.named_scope("dispatch"):
        resid, message = dispatch(keep_own, from_core, from_z, expert_gain, place)
        arrived = lax.all_to_all(message, everyone, 0, 0, tiled=True)
    with jax.named_scope("router"):
        part = chosen_logits(resid, expert_gain, router, choice)
        parts = [part] + [lax.ppermute(part, "sec", pairs) for pairs in (core, z_far, both)]
    with jax.named_scope("gates"):
        gates = gate_matrix(parts, where, experts)
    with jax.named_scope("experts"):
        result = run_expert(arrived, expert_gain, weights)
        returned = lax.all_to_all(result, everyone, 0, 0, tiled=True)
    with jax.named_scope("combine"):
        return combine(alive, resid, gates, returned, users)


def solution(mesh):
    in_specs = (
        P("dp", None, None),
        P("dp", None),
        P("dp", None),
        P("dp"),
        P("dp", None, None),
        P(),
        P(None, "sec"),
        P(None, "sec"),
        P(None, "sec"),
        P("sec", None),
        P("dp", None, "sec"),
        P("dp", None, "sec"),
        P("dp", None, None, "sec"),
        P("dp", None, None, "sec"),
        P(),
        P(),
        P("dp", None, "sec"),
        P("dp", None, "sec"),
        P("dp", "sec", None),
    )
    out_specs = P("dp", None, "sec")
    return jax.shard_map(
        on_device, mesh=mesh, in_specs=in_specs, out_specs=out_specs, check_vma=False
    )
```

```python
import functools
import math

import jax
import jax.numpy as jnp
from jax import lax
from jax.experimental import pallas as pl
from jax.experimental.pallas import tpu as pltpu
from jax.sharding import PartitionSpec as P

HD = 128
EPSILON = 1e-05
BF16 = jnp.bfloat16
F32 = jnp.float32
MIB = 1024 * 1024
WHOLE = pl.BlockSpec(memory_space=pltpu.VMEM)
IN_HBM = pl.BlockSpec(memory_space=pl.ANY)


def mm(a, b):
    return jnp.dot(a, b, preferred_element_type=F32)


def mm_nt(a, b):
    return lax.dot_general(a, b, (((1,), (1,)), ((), ())), preferred_element_type=F32)


def iota(shape, dim):
    return lax.broadcasted_iota(jnp.int32, shape, dim)


def call(kernel, out, in_specs, vmem_mib, flops, nbytes, scratch=(), transcendentals=0, out_specs=None):
    return pl.pallas_call(
        kernel,
        out_shape=out,
        in_specs=in_specs,
        out_specs=jax.tree.map(lambda _: WHOLE, out) if out_specs is None else out_specs,
        scratch_shapes=list(scratch),
        compiler_params=pltpu.CompilerParams(vmem_limit_bytes=vmem_mib * MIB),
        cost_estimate=pl.CostEstimate(
            flops=flops, bytes_accessed=nbytes, transcendentals=transcendentals
        ),
    )


class Loads:
    def __init__(self, sems):
        self.sems = sems
        self.copies, self.count = {}, 0

    def start(self, name, *pieces):
        for src, dst in pieces:
            copy = pltpu.make_async_copy(src, dst, self.sems.at[self.count])
            copy.start()
            self.copies.setdefault(name, []).append(copy)
            self.count += 1

    def start_rows(self, name, src, dst, pieces):
        size = dst.shape[0] // pieces
        cuts = [pl.ds(n * size, size) for n in range(pieces)]
        self.start(name, *[(src.at[cut], dst.at[cut]) for cut in cuts])

    def wait(self, name):
        for copy in self.copies[name]:
            copy.wait()


def attention_kernel(
    kept_h, parent_h, gain_h, state_h, wq_h, wk_h, wv_h, wo_h, kh_h, vh_h, dk_h, dv_h,
    keep_own, keep_other, send,
    kept, parent, gain, st, sq, wq, wk, wv, wo, kh, vh, dk, dv, nrm, q, k, v, own, att, scores, sems,
):
    users, slots, width = st.shape
    history = kh.shape[1]
    feat = wq.shape[1]
    heads = feat // HD
    sec = lax.axis_index("sec")
    z, c = sec // 2, sec % 2

    def quarter(n):
        return pl.ds(pl.multiple_of(n * feat, feat), feat)

    loads = Loads(sems)
    loads.start("small", (kept_h, kept), (parent_h, parent), (gain_h, gain))
    for u in range(users):
        loads.start_rows(("st", u), state_h.at[u], st.at[u], 2)
    loads.start_rows("wq", wq_h, wq, 2)
    loads.start_rows("wk", wk_h, wk, 2)
    loads.start_rows("wv", wv_h, wv, 2)
    for u in range(users):
        loads.start(
            ("past", u),
            (dk_h.at[u], dk.at[u]),
            (dv_h.at[u], dv.at[u]),
        )
        loads.start_rows(("kh", u), kh_h.at[u], kh.at[u], 2)
        loads.start_rows(("vh", u), vh_h.at[u], vh.at[u], 2)
    loads.start_rows("wo", wo_h, wo, 2)

    loads.wait("small")
    picks = []
    for u in range(users):
        rows = pl.ds(u * slots, slots)
        picks.append((iota((slots, slots), 0) == kept[u : u + 1, :]).astype(F32).T.astype(BF16))
        loads.wait(("st", u))
        xu = mm(picks[u], st[u])
        mean = jnp.mean(xu * xu, axis=-1, keepdims=True)
        nrm[rows, :] = (xu * lax.rsqrt(mean + EPSILON) * gain[...]).astype(BF16)
    loads.wait("wq")
    q[...] = (mm(nrm[...], wq[...]) * (HD ** (-0.5) * math.log2(math.e))).astype(BF16)
    loads.wait("wk")
    k[...] = mm(nrm[...], wk[...]).astype(BF16)
    loads.wait("wv")
    v[...] = mm(nrm[...], wv[...]).astype(BF16)

    steps = dk.shape[2]
    chunk = 512
    chunks = [slice(a, a + chunk) for a in range(0, history, chunk)]
    group = 2
    tall, wide = group * slots, group * HD
    sets = [(u, h) for u in range(users) for h in range(0, heads, group)]
    past = {}
    ready = {}

    def stack(f):
        return jnp.concatenate([f(slice(m * HD, (m + 1) * HD)) for m in range(group)], axis=0)

    for n in range(len(sets) + 1):
        if n < len(sets):
            u, h = sets[n]
            rows = pl.ds(u * slots, slots)
            cols = slice(h * HD, h * HD + wide)
            if h == 0:
                loads.wait(("past", u))
                past[u] = []
                flat = [t[u].reshape(slots * steps, feat) for t in (dk, dv)]
                for s in range(steps):
                    hot = iota((steps * slots, slots), 0) == parent[u : u + 1, :] * steps + s
                    pick = hot.astype(F32).T.astype(BF16)
                    past[u].append(tuple(mm(pick, t) for t in flat))
                loads.wait(("kh", u))
                loads.wait(("vh", u))
            qs = q[rows, cols]
            blank = jnp.zeros((slots, HD), BF16)
            diagonal = jnp.concatenate(
                [
                    jnp.concatenate(
                        [qs[:, m * HD : (m + 1) * HD] if m == at else blank for m in range(group)], axis=1
                    )
                    for at in range(group)
                ],
                axis=0,
            )
            qf = qs.astype(F32)
            more = []
            for p in [p for p, _ in past[u]] + [k[rows, :].astype(F32)]:
                both = qf * p[:, cols]
                more.append(stack(lambda m: jnp.sum(both[:, m], axis=-1, keepdims=True)))
            high = jnp.full((tall, HD), -jnp.inf, F32)
        if n > 0:
            u0, h0, more0, top = ready.pop(n - 1)
            rows0 = pl.ds(u0 * slots, slots)
            cols0 = slice(h0 * HD, h0 * HD + wide)
            mass = jnp.zeros((tall, HD), F32)
            mixed = jnp.zeros((tall, wide), F32)
        for at in chunks:
            if n < len(sets):
                s = mm_nt(diagonal, kh[u, at, cols])
                scores[n % 2, :, at] = s
                for a in range(0, chunk, HD):
                    high = jnp.maximum(high, s[:, a : a + HD])
            if n > 0:
                e = jnp.exp2(scores[(n - 1) % 2, :, at] - top)
                for a in range(0, chunk, HD):
                    mass = mass + e[:, a : a + HD]
                mixed = mixed + mm(e.astype(BF16), vh[u0, at, cols0])
        if n < len(sets):
            peak = jnp.max(high, axis=-1, keepdims=True)
            for s in more:
                peak = jnp.maximum(peak, s)
            ready[n] = (u, h, more, peak)
        if n > 0:
            total = jnp.sum(mass, axis=-1, keepdims=True)
            mixed = jnp.concatenate(
                [mixed[m * slots : (m + 1) * slots, m * HD : (m + 1) * HD] for m in range(group)], axis=0
            )
            values = [p[:, cols0] for _, p in past[u0]] + [v[rows0, cols0].astype(F32)]
            for s, value in zip(more0, values):
                e = jnp.exp2(s - top)
                total = total + e
                mixed = mixed + e * stack(lambda m: value[:, m])
            mixed = (mixed / total).astype(BF16)
            att[rows0, cols0] = jnp.concatenate(
                [mixed[m * slots : (m + 1) * slots] for m in range(group)], axis=1
            )

    for u in range(users):
        own[pl.ds(u * slots, slots), :] = mm(picks[u], st[u, :, quarter(sec)]).astype(BF16)
    loads.wait("wo")
    keep_own[...] = mm(att[...], wo[:, quarter(sec)]) + own[...].astype(F32)
    keep_other[...] = mm(att[...], wo[:, quarter(2 * (1 - z) + c)])
    send[:, :feat] = mm(att[...], wo[:, quarter(2 * z + 1 - c)]).astype(BF16)
    send[:, feat:] = mm(att[...], wo[:, quarter(2 * (1 - z) + 1 - c)]).astype(BF16)


def routing_kernel(alive, choice, place, where):
    users, top, slots = choice.shape
    rows = users * slots
    lane = iota((1, slots), 1)
    live = jnp.concatenate([lane < alive[:, u : u + 1] for u in range(users)], axis=1)
    experts = place.shape[0] // (6 * 8)
    earlier = (iota((rows, rows), 0) < iota((rows, rows), 1)).astype(F32).astype(BF16)
    base = jnp.zeros((experts, 1), F32)
    main, extra = [], []
    for t in range(top):
        e = jnp.concatenate([choice[u, t : t + 1, :] for u in range(users)], axis=1)
        hot = ((iota((experts, rows), 0) == e) & live).astype(F32)
        before = mm(hot.astype(BF16), earlier)
        rank = jnp.sum(hot * (before + base), axis=0, keepdims=True).astype(jnp.int32)
        base = base + jnp.sum(hot, axis=1, keepdims=True)
        over = rank - 16
        main.append(
            jnp.where(live & (rank < 16), (rank >> 3) * (experts * 8) + e * 8 + (rank & 7), -1)
        )
        extra.append(
            jnp.where(live & (rank >= 16), (over >> 2) * (experts * 8) + e * 8 + (over & 3), -8)
        )
    span = 2 * experts * 8
    index = iota((span, rows), 0)
    for part, (a, b) in enumerate(
        ((main[0], main[1]), (extra[0], extra[1]), (extra[0] + 4, extra[1] + 4))
    ):
        hit = (index == a) | (index == b)
        place[part * span : (part + 1) * span, :] = hit.astype(F32).astype(BF16)
    blank = jnp.zeros((4, rows), jnp.int32)
    where[...] = jnp.concatenate(main + extra + [blank], axis=0)


def dispatch_kernel(keep, from_core, from_z, gain, place, resid, message, block, sems):
    feat = keep.shape[1]
    half = feat // 2
    span = place.shape[0] // 3
    part = span // 2
    sec = lax.axis_index("sec")
    r = keep[...] + from_core[:, :feat].astype(F32) + from_z[...].astype(F32)
    scaled = (r * gain[:, pl.ds(pl.multiple_of(sec * feat, feat), feat)]).astype(BF16)
    copies = []
    for n in range(2):
        rows = slice(n * part, (n + 1) * part)
        block[rows, :feat] = mm(place[rows, :], scaled).astype(BF16)
        folded = mm(place[span + n * part : span + (n + 1) * part, :], scaled[:, :half])
        folded = folded + mm(
            place[2 * span + n * part : 2 * span + (n + 1) * part, :], scaled[:, half:]
        )
        block[rows, feat:] = folded.astype(BF16)
        for z in range(2):
            copies.append(
                pltpu.make_async_copy(
                    block.at[pl.ds(n * part, part)],
                    message.at[pl.ds(z * span + n * part, part)],
                    sems.at[len(copies)],
                )
            )
            copies[-1].start()
    resid[...] = r
    for copy in copies:
        copy.wait()


def router_kernel(resid, gain, router, choice, part):
    users, top, slots = choice.shape
    rows = users * slots
    feat = resid.shape[1]
    experts = router.shape[0]
    sec = lax.axis_index("sec")
    cols = pl.ds(pl.multiple_of(sec * feat, feat), feat)
    r = resid[...]
    scaled = (r * gain[:, cols]).astype(BF16)
    logits = mm_nt(router[:, cols], scaled)
    out = []
    for t in range(top):
        e = jnp.concatenate([choice[u, t : t + 1, :] for u in range(users)], axis=1)
        hot = (iota((experts, rows), 0) == e).astype(F32)
        out.append(jnp.sum(hot * logits, axis=0, keepdims=True))
    squares = lax.dot_general(
        jnp.ones((8, feat), F32), r * r, (((1,), (1,)), ((), ())),
        precision=lax.Precision.HIGHEST, preferred_element_type=F32,
    )
    part[...] = jnp.concatenate(out + [squares[: 8 - top]], axis=0)


def gate_kernel(p0, p1, p2, p3, where, gates):
    rows = where.shape[1]
    total = (p0[...] + p1[...]) + (p2[...] + p3[...])
    width = gates.shape[1] // 3 * 4
    scale = lax.rsqrt(total[2:3] / width + EPSILON)
    sig = [1.0 / (1.0 + jnp.exp(-(total[t : t + 1] * scale))) for t in range(2)]
    weight = [s / (sig[0] + sig[1]) for s in sig]
    span = gates.shape[1] // 3
    index = iota((span, rows), 0)
    for part, shift in enumerate((0, 0, 4)):
        first = 0 if part == 0 else 2
        g = jnp.where(index == where[first : first + 1, :] + shift, weight[0], 0.0)
        g = jnp.where(index == where[first + 1 : first + 2, :] + shift, weight[1], g)
        gates[:, part * span : (part + 1) * span] = g.T.astype(BF16)


def unfold(folded):
    rows, width = folded.shape
    pair = folded.astype(F32).reshape(rows // 16, 2, 8, width)
    a, b = pair[:, 0], pair[:, 1]
    first = iota(a.shape, 1) < 4
    left = jnp.where(first, a, pltpu.roll(b, 4, 1))
    right = jnp.where(first, pltpu.roll(a, 4, 1), b)
    return [t.reshape(rows // 2, width).astype(BF16) for t in (left, right)]


def fold(left, right):
    rows, width = left.shape
    left, right = (t.reshape(rows // 8, 8, width) for t in (left, right))
    first = iota(left.shape, 1) < 4
    a = jnp.where(first, left, pltpu.roll(right, 4, 1))
    b = jnp.where(first, pltpu.roll(left, 4, 1), right)
    return jnp.stack([a, b], axis=1).reshape(rows * 2, width)


def expert_kernel(
    arrived, gain, wg0_h, wu0_h, wd0_h, wg1_h, wu1_h, wd1_h, message,
    wg0, wu0, wg1, wu1, wd, x, act, block, sems, out_sems,
):
    width, hidden = wg0.shape
    quarters = 4
    feat = width // quarters
    half = feat // 2
    part = arrived.shape[0] // quarters
    loads = Loads(sems)
    for n, (src, dst) in enumerate(((wg0_h, wg0), (wu0_h, wu0), (wg1_h, wg1), (wu1_h, wu1))):
        loads.start_rows(n, src.at[0], dst, 4)
    loads.start_rows(4, wd0_h.at[0], wd.at[pl.ds(0, hidden)], 4)
    loads.start_rows(5, wd1_h.at[0], wd.at[pl.ds(hidden, hidden)], 4)
    for p in range(quarters):
        rows = slice(p * part, (p + 1) * part)
        x[:part, p * feat : (p + 1) * feat] = arrived[rows, :feat]
        for n, piece in enumerate(unfold(arrived[rows, feat:])):
            at = p * feat + n * half
            x[part:, at : at + half] = piece
    plain = x[...].astype(F32) * (1.0 / gain[...])
    scale = lax.rsqrt(jnp.mean(plain * plain, axis=-1, keepdims=True) + EPSILON)
    for n, (wg, wu) in enumerate(((wg0, wu0), (wg1, wu1))):
        if n == 0:
            for copy in loads.copies[0][:2]:
                copy.wait()
            g = mm(x[:, : width // 2], wg[: width // 2, :])
            for copy in loads.copies[0][2:]:
                copy.wait()
            g = (g + mm(x[:, width // 2 :], wg[width // 2 :, :])) * scale
        else:
            loads.wait(2 * n)
            g = mm(x[...], wg[...]) * scale
        loads.wait(2 * n + 1)
        u = mm(x[...], wu[...]) * scale
        act[:, n * hidden : (n + 1) * hidden] = (g / (1.0 + jnp.exp(-g)) * u).astype(BF16)
    loads.wait(4)
    loads.wait(5)
    copies = []
    for p in range(quarters):
        cols = slice(p * feat, (p + 1) * feat)
        rows = slice(p * part, (p + 1) * part)
        y = mm(act[...], wd[:, cols])
        block[rows, :feat] = y[:part].astype(BF16)
        block[rows, feat:] = fold(y[part:, :half], y[part:, half:]).astype(BF16)
        for n in range(4):
            here = pl.ds(p * part + n * (part // 4), part // 4)
            copies.append(
                pltpu.make_async_copy(block.at[here], message.at[here], out_sems.at[len(copies)])
            )
            copies[-1].start()
    for copy in copies:
        copy.wait()


def combine_kernel(alive, resid, gates, arrived, out):
    users, slots, feat = out.shape
    span = gates.shape[1] // 3

    def bring(part, cols):
        g = gates[:, part * span : (part + 1) * span]
        return mm(jnp.concatenate([g, g], axis=1), arrived[:, cols])

    main = bring(0, slice(0, feat))
    tail = slice(feat, arrived.shape[1])
    total = resid[...] + main + jnp.concatenate([bring(1, tail), bring(2, tail)], axis=1)
    for u in range(users):
        live = iota((slots, feat), 0) < alive[:, u : u + 1]
        rows = slice(u * slots, (u + 1) * slots)
        out[u] = jnp.where(live, total[rows], 0.0).astype(BF16)


struct = jax.ShapeDtypeStruct


def in_hbm(a):
    return pltpu.with_memory_space_constraint(a, pltpu.HBM)


def attention(kept, parent, gain, state, wq, wk, wv, wo, keys, values, past_keys, past_values):
    users, slots, width = state.shape
    feat = wq.shape[1]
    history = keys.shape[1]
    steps = past_keys.shape[2]
    rows = users * slots
    return call(
        attention_kernel,
        (struct((rows, feat), F32), struct((rows, feat), F32), struct((rows, 2 * feat), BF16)),
        [IN_HBM] * 12,
        40,
        3_300_000_000,
        20_000_000,
        [
            pltpu.VMEM(kept.shape, jnp.int32),
            pltpu.VMEM(parent.shape, jnp.int32),
            pltpu.VMEM(gain.shape, F32),
            pltpu.VMEM((users, slots, width), BF16),
            pltpu.VMEM((users, slots, feat), BF16),
            pltpu.VMEM((width, feat), BF16),
            pltpu.VMEM((width, feat), BF16),
            pltpu.VMEM((width, feat), BF16),
            pltpu.VMEM((feat, width), BF16),
            pltpu.VMEM((users, history, feat), BF16),
            pltpu.VMEM((users, history, feat), BF16),
            pltpu.VMEM(past_keys.shape, BF16),
            pltpu.VMEM(past_keys.shape, BF16),
            pltpu.VMEM((rows, width), BF16),
            pltpu.VMEM((rows, feat), BF16),
            pltpu.VMEM((rows, feat), BF16),
            pltpu.VMEM((rows, feat), BF16),
            pltpu.VMEM((rows, feat), BF16),
            pltpu.VMEM((rows, feat), BF16),
            pltpu.VMEM((2, 2 * slots, history), F32),
            pltpu.SemaphoreType.DMA((20 + 12 * users,)),
        ],
        2_200_000,
    )(
        *[
            in_hbm(a)
            for a in (
                kept, parent, gain, state, wq, wk, wv, wo, keys, values, past_keys, past_values,
            )
        ]
    )


def route(alive, choice, experts):
    users, top, slots = choice.shape
    rows = users * slots
    return call(
        routing_kernel,
        (struct((6 * 8 * experts, rows), BF16), struct((8, rows), jnp.int32)),
        [WHOLE] * 2,
        16,
        10_000_000,
        1_000_000,
    )(alive, choice)


def dispatch(keep, from_core, from_z, gain, place):
    rows, feat = keep.shape
    span = place.shape[0] // 3
    return call(
        dispatch_kernel,
        (struct((rows, feat), F32), pltpu.HBM((2 * span, feat * 3 // 2), BF16)),
        [WHOLE] * 5,
        16,
        300_000_000,
        4_000_000,
        [pltpu.VMEM((span, feat * 3 // 2), BF16), pltpu.SemaphoreType.DMA((4,))],
        out_specs=(WHOLE, IN_HBM),
    )(keep, from_core, from_z, gain, place)


def chosen_logits(resid, gain, router, choice):
    return call(
        router_kernel, struct((8, resid.shape[0]), F32), [WHOLE] * 4, 16, 30_000_000, 1_000_000
    )(resid, gain, router, choice)


def gate_matrix(parts, where, experts):
    return call(
        gate_kernel,
        struct((where.shape[1], 6 * 8 * experts), BF16),
        [WHOLE] * 5,
        16,
        3_000_000,
        1_000_000,
    )(*parts, where)


def run_expert(arrived, gain, weights):
    _, width, hidden = weights[0].shape
    rows = arrived.shape[0] // 8 * 3
    return call(
        expert_kernel,
        pltpu.HBM(arrived.shape, BF16),
        [WHOLE] * 2 + [IN_HBM] * 6,
        40,
        4_800_000_000,
        16_000_000,
        [
            pltpu.VMEM((width, hidden), BF16),
            pltpu.VMEM((width, hidden), BF16),
            pltpu.VMEM((width, hidden), BF16),
            pltpu.VMEM((width, hidden), BF16),
            pltpu.VMEM((2 * hidden, width), BF16),
            pltpu.VMEM((rows, width), BF16),
            pltpu.VMEM((rows, 2 * hidden), BF16),
            pltpu.VMEM(arrived.shape, BF16),
            pltpu.SemaphoreType.DMA((24,)),
            pltpu.SemaphoreType.DMA((16,)),
        ],
        400_000,
        IN_HBM,
    )(arrived, gain, *[in_hbm(w) for w in weights])


def combine(alive, resid, gates, returned, users):
    rows, feat = resid.shape
    return call(
        combine_kernel,
        struct((users, rows // users, feat), BF16),
        [WHOLE] * 4,
        24,
        600_000_000,
        4_000_000,
    )(alive, resid, gates, returned)


def on_device(
    candidate_hidden_states,
    kept_candidate_index,
    slot_parent_beam,
    alive_slot_counts,
    slot_expert_index,
    attention_norm_gain,
    query_projection_weight,
    key_projection_weight,
    value_projection_weight,
    attention_output_weight,
    history_event_keys,
    history_event_values,
    decoded_beam_keys,
    decoded_beam_values,
    expert_norm_gain,
    router_projection_weight,
    expert_gate_weight,
    expert_up_weight,
    expert_down_weight,
):
    users, slots, width = candidate_hidden_states.shape
    feat = query_projection_weight.shape[1]
    experts = router_projection_weight.shape[1]
    core = [(s, s ^ 1) for s in range(4)]
    z_far = [(s, s ^ 2) for s in range(4)]
    both = [(s, s ^ 3) for s in range(4)]
    everyone = ("sec", "dp")

    attention_gain = attention_norm_gain.reshape(1, width)
    expert_gain = expert_norm_gain.reshape(1, width)
    alive = alive_slot_counts.reshape(1, users)
    choice = jnp.swapaxes(slot_expert_index, 1, 2)
    router = router_projection_weight.T

    with jax.named_scope("attention"):
        keep_own, keep_other, send = attention(
            kept_candidate_index, slot_parent_beam, attention_gain, candidate_hidden_states,
            query_projection_weight, key_projection_weight, value_projection_weight,
            attention_output_weight, history_event_keys, history_event_values,
            decoded_beam_keys, decoded_beam_values,
        )
    with jax.named_scope("head_sum"):
        from_core = lax.ppermute(send, "sec", core)
        to_z = (keep_other + from_core[:, feat:].astype(F32)).astype(BF16)
        from_z = lax.ppermute(to_z, "sec", z_far)
    with jax.named_scope("routing"):
        place, where = route(alive, choice, experts)
    with jax.named_scope("sibling_weights"):
        weights = [expert_gate_weight, expert_up_weight, expert_down_weight]
        late = lax.optimization_barrier((*weights, where))[:3]
        weights = weights + [lax.ppermute(w, "sec", core) for w in late]
    with jax.named_scope("dispatch"):
        resid, message = dispatch(keep_own, from_core, from_z, expert_gain, place)
        arrived = lax.all_to_all(message, everyone, 0, 0, tiled=True)
    with jax.named_scope("router"):
        part = chosen_logits(resid, expert_gain, router, choice)
        parts = [part] + [lax.ppermute(part, "sec", pairs) for pairs in (core, z_far, both)]
    with jax.named_scope("gates"):
        gates = gate_matrix(parts, where, experts)
    with jax.named_scope("experts"):
        result = run_expert(arrived, expert_gain, weights)
        returned = lax.all_to_all(result, everyone, 0, 0, tiled=True)
    with jax.named_scope("combine"):
        return combine(alive, resid, gates, returned, users)


def solution(mesh):
    in_specs = (
        P("dp", None, None),
        P("dp", None),
        P("dp", None),
        P("dp"),
        P("dp", None, None),
        P(),
        P(None, "sec"),
        P(None, "sec"),
        P(None, "sec"),
        P("sec", None),
        P("dp", None, "sec"),
        P("dp", None, "sec"),
        P("dp", None, None, "sec"),
        P("dp", None, None, "sec"),
        P(),
        P(),
        P("dp", None, "sec"),
        P("dp", None, "sec"),
        P("dp", "sec", None),
    )
    out_specs = P("dp", None, "sec")
    return jax.shard_map(
        on_device, mesh=mesh, in_specs=in_specs, out_specs=out_specs, check_vma=False
    )
```
